32 devices in a mesh: batch: 8 (over z, y), temp: 4 (over x, core).
Axes of the slice: x: 2, y: 2, z: 4, core: 2. Of those that a mesh axis runs over, the one named last changes fastest.
Arguments:
- embeddings: bfloat16 [2, 1024, 1152], P(None, 'batch'), may hold values from -40 to 40
- spread_code: int32 [1024], replicated, may hold values from 0 to 3
- level_index: int32 [4], P('temp'), may hold values from 0 to 5
Outputs:
- grad_student: float32 [1024, 1152], P(('batch', 'temp'))
- row_loss: float32 [1024], P(('batch', 'temp'))
The draws below stay inside these ranges and needn't reach their ends.
Inputs may be any that keep to these rules, and one draw needn't show every extreme that they name: `spread_code`: spread codes. `level_index`: temperature codes.
All inputs are finite; a program needn't handle non-finite values.
Results may differ from the reference program's by a relative error of at most 0.0075.
Values may be sent and summed in bfloat16 or wider, within the bound.
No kernel may reach another device: no remote copies, remote signals or barrier semaphores. Data moves between devices by JAX's collectives and lax.ppermute only.
A program may use at most 192 MiB of HBM per device.

```python
import jax
import jax.numpy as jnp
from jax import lax

D = 1152
ROW_DEV = 128
LEVEL_MAX = 6
CODES = 4
ROWS = 1024
LEVELS = 4


def draw_embeddings(key, part):
    first = jax.random.fold_in(key, 0)
    return jax.random.truncated_normal(first, -5.0, 5.0, (2, ROWS, D), jnp.float32).astype(jnp.bfloat16)


def set_ends(values, rng, smallest, largest):
    longest = values.shape.index(max(values.shape))
    spots = []
    for shift in (0, 1):
        where = [jax.random.randint(jax.random.fold_in(rng, axis), (), 0, length) for axis, length in enumerate(values.shape)]
        where[longest] = (where[longest] + shift) % values.shape[longest]
        spots.append(tuple(where))
    return values.at[spots[0]].set(smallest).at[spots[1]].set(largest)


def setup_inputs(seed: int = 0) -> dict:
    streams_of = jax.random.split(jax.random.key(seed), 4)
    return {
        "embeddings": draw_embeddings(jax.random.fold_in(streams_of[3], 71), 0),
        "spread_code": set_ends(jax.random.randint(streams_of[1], (ROWS,), 0, CODES), jax.random.fold_in(streams_of[1], 1), 0, CODES - 1).astype(jnp.int32),
        "level_index": set_ends(jax.random.randint(streams_of[2], (LEVELS,), 0, LEVEL_MAX), jax.random.fold_in(streams_of[2], 1), 0, LEVEL_MAX - 1).astype(jnp.int32),
    }


WEIGHT = 16.0
NEG = -1e+30

def widths(codes, level, width):
    return jnp.exp2(0.5 * (codes.astype(jnp.float32) - level.astype(jnp.float32))) / jnp.sqrt(jnp.float32(width))

def logsum(row_beta, gram, self_pair):
    logits = jnp.where(self_pair, NEG, row_beta[:, None] * gram)
    top = lax.optimization_barrier(jnp.max(logits, axis=1))
    return top + jnp.log(lax.optimization_barrier(jnp.sum(jnp.exp(logits - top[:, None]), axis=1)))

def mixing(row_beta, col_beta, row_lt, row_ls, col_lt, col_ls, gt, gs, self_pair):
    pr = jnp.exp(jnp.where(self_pair, NEG, row_beta[:, None] * gt) - row_lt[:, None])
    qr = jnp.exp(jnp.where(self_pair, NEG, row_beta[:, None] * gs) - row_ls[:, None])
    pc = jnp.exp(jnp.where(self_pair, NEG, col_beta[None, :] * gt) - col_lt[None, :])
    qc = jnp.exp(jnp.where(self_pair, NEG, col_beta[None, :] * gs) - col_ls[None, :])
    return (WEIGHT * (row_beta[:, None] * (qr - pr) + col_beta[None, :] * (qc - pc))).astype(jnp.bfloat16)

def reference(embeddings, spread_code, level_index):
    teacher = embeddings[0]
    student = embeddings[1]
    count = ROWS // ROW_DEV
    starts = jnp.arange(count, dtype=jnp.int32) * ROW_DEV
    columns = jnp.arange(ROWS, dtype=jnp.int32)
    betas = [widths(spread_code, level_index[k], D) for k in range(LEVELS)]

    def block_grams(start):
        t_rows = lax.dynamic_slice_in_dim(teacher, start, ROW_DEV, 0)
        s_rows = lax.dynamic_slice_in_dim(student, start, ROW_DEV, 0)
        gt = jnp.dot(t_rows, teacher.T, preferred_element_type=jnp.float32)
        gs = jnp.dot(s_rows, student.T, preferred_element_type=jnp.float32)
        own = start + jnp.arange(ROW_DEV, dtype=jnp.int32)
        return (gt, gs, own[:, None] == columns[None, :])

    def logsums(start):
        gt, gs, self_pair = block_grams(start)
        result = []
        for k in range(LEVELS):
            row_beta = lax.dynamic_slice_in_dim(betas[k], start, ROW_DEV)
            result.append(jnp.stack([logsum(row_beta, gt, self_pair), logsum(row_beta, gs, self_pair)]))
        return jnp.stack(result)
    sums = lax.map(logsums, starts)
    sums = jnp.transpose(sums, (1, 2, 0, 3)).reshape(LEVELS, 2, ROWS)

    def gradient(start):
        gt, gs, self_pair = block_grams(start)
        grad = jnp.zeros((ROW_DEV, D), jnp.float32)
        loss = jnp.zeros((ROW_DEV,), jnp.float32)
        for k in range(LEVELS):
            row_beta = lax.dynamic_slice_in_dim(betas[k], start, ROW_DEV)
            row_lt = lax.dynamic_slice_in_dim(sums[k, 0], start, ROW_DEV)
            row_ls = lax.dynamic_slice_in_dim(sums[k, 1], start, ROW_DEV)
            mix = mixing(row_beta, betas[k], row_lt, row_ls, sums[k, 0], sums[k, 1], gt, gs, self_pair)
            grad = grad + jnp.dot(mix, student, preferred_element_type=jnp.float32)
            pr = jnp.exp(jnp.where(self_pair, NEG, row_beta[:, None] * gt) - row_lt[:, None])
            loss = loss + lax.optimization_barrier(jnp.sum(pr * (row_beta[:, None] * (gt - gs)), axis=1)) - row_lt + row_ls
        return (grad, loss)
    grads, losses = lax.map(gradient, starts)
    return (grads.reshape(ROWS, D), losses.reshape(ROWS))
```

```python
import functools

import jax
import jax.numpy as jnp
from jax import lax
from jax.experimental import pallas as pl
from jax.experimental.pallas import tpu as pltpu
from jax.sharding import PartitionSpec as P

WEIGHT = 16.0
NEG = -1e30
LOG2E = 1.4426950408889634
TILE = 256
CHUNK = 128
SPAN = 1024
ALL = ("batch", "temp")


def loop(count, body):
    if count <= 8:
        for i in range(count):
            body(i)
    else:
        lax.fori_loop(0, count, lambda i, c: (body(i), c)[1], 0)


def at(i, size):
    return pl.ds(i * size if isinstance(i, int) else pl.multiple_of(i * size, size), size)


def column_betas(codes, level, width):
    return jnp.exp2(0.5 * (codes.astype(jnp.float32) - level.astype(jnp.float32))) / jnp.sqrt(
        jnp.float32(width)
    )


def stats_kernel(count, rows, scalars, codes, *refs):
    pieces, refs = refs[:count], refs[count:]
    if count == 1:
        whole, (stats, strip, gram) = pieces[0], refs
    else:
        stats, strip, whole, gram = refs
        for p, piece in enumerate(pieces):
            start = pl.multiple_of(scalars[2 + p], 64)
            whole[pl.ds(start, piece.shape[0]), :] = piece[...]
    levels = scalars.shape[0] - 2 - count
    total, width = whole.shape

    def tile(j):
        cols = at(j, TILE)
        gram[...] = lax.dot_general(
            whole[...], whole[cols, :], (((1,), (1,)), ((), ())), preferred_element_type=jnp.float32
        )
        square = gram[cols, :]
        own = lax.broadcasted_iota(jnp.int32, square.shape, 0) == lax.broadcasted_iota(
            jnp.int32, square.shape, 1
        )
        gram[cols, :] = jnp.where(own, NEG, square)
        strip[:, cols] = gram[pl.ds(pl.multiple_of(scalars[0], rows), rows), :]
        code = codes[:, cols]
        scale = [
            column_betas(code, scalars[2 + count + k], width) * LOG2E for k in range(levels)
        ]
        steps = total // CHUNK

        def top(i, best):
            return jnp.maximum(best, jnp.max(gram[at(i, CHUNK), :], axis=0, keepdims=True))

        best = jnp.full((1, TILE), NEG, jnp.float32)
        if steps <= 8:
            for i in range(steps):
                best = top(i, best)
        else:
            best = lax.fori_loop(0, steps, top, best)

        def add(i, sums):
            d = gram[at(i, CHUNK), :] - best
            return tuple(
                s + jnp.sum(jnp.exp2(d * b), axis=0, keepdims=True) for s, b in zip(sums, scale)
            )

        sums = tuple(jnp.zeros((1, TILE), jnp.float32) for _ in range(levels))
        if steps <= 8:
            for i in range(steps):
                sums = add(i, sums)
        else:
            sums = lax.fori_loop(0, steps, add, sums)
        stats[0:1, cols] = best
        for k in range(levels):
            stats[1 + k : 2 + k, cols] = sums[k]
        stats[levels + 1 : levels + 2, cols] = code.astype(jnp.float32)
        if levels + 2 < stats.shape[0]:
            stats[levels + 2 :, cols] = jnp.zeros((stats.shape[0] - levels - 2, TILE), jnp.float32)

    loop(total // TILE, tile)


def mix_kernel(rows, block, scalars, s_stats, s_strip, t_stats, t_strip, student, out, turned):
    levels = scalars.shape[0] - 2
    total, width = student.shape
    half = rows // 2
    own = pl.ds(pl.multiple_of(scalars[1], block), block)
    turned[0] = s_stats[:, own].T
    turned[1] = t_stats[:, own].T
    mine = pl.ds(pl.multiple_of(scalars[0] - scalars[1], rows), rows)
    s_row, t_row = turned[0, mine, :], turned[1, mine, :]
    root = jnp.sqrt(jnp.float32(width))

    def beta(code, k):
        return jnp.exp2(0.5 * (code - scalars[2 + k].astype(jnp.float32))) / root

    row_beta = [beta(s_row[:, levels + 1 : levels + 2], k) for k in range(levels)]
    span = min(SPAN, total)
    loss = jnp.zeros((rows, 1), jnp.float32)
    grad = jnp.zeros((rows, width), jnp.float32)

    def piece(i, carry):
        loss, grad = carry
        cols = at(i, span)
        gs, gt = s_strip[:, cols], t_strip[:, cols]
        code = s_stats[levels + 1 : levels + 2, cols]
        s_from_row, t_from_row = gs - s_row[:, 0:1], gt - t_row[:, 0:1]
        s_from_col, t_from_col = gs - s_stats[0:1, cols], gt - t_stats[0:1, cols]
        gap = gt - gs
        mix = None
        for k in range(levels):
            a = row_beta[k]
            b = beta(code, k)
            a2, b2 = a * LOG2E, b * LOG2E
            pr = jnp.exp2(t_from_row * a2) * (a / t_row[:, 1 + k : 2 + k])
            qr = jnp.exp2(s_from_row * a2) * (a / s_row[:, 1 + k : 2 + k])
            pc = jnp.exp2(t_from_col * b2) * (b / t_stats[1 + k : 2 + k, cols])
            qc = jnp.exp2(s_from_col * b2) * (b / s_stats[1 + k : 2 + k, cols])
            loss = loss + jnp.sum(pr * gap, axis=1, keepdims=True)
            term = (qr - pr) + (qc - pc)
            mix = term if mix is None else mix + term
        grad = grad + jnp.dot(
            (WEIGHT * mix).astype(jnp.bfloat16),
            student[cols, :],
            preferred_element_type=jnp.float32,
        )
        return loss, grad

    if total == span:
        loss, grad = piece(0, (loss, grad))
    else:
        loss, grad = lax.fori_loop(0, total // span, piece, (loss, grad))
    for k in range(levels):
        loss = loss + (
            row_beta[k] * (s_row[:, 0:1] - t_row[:, 0:1])
            + jnp.log(s_row[:, 1 + k : 2 + k])
            - jnp.log(t_row[:, 1 + k : 2 + k])
        )
    line = jnp.broadcast_to(loss, (rows, 128)).T
    for h in range(2):
        out[h, 0:half, :] = grad[h * half : (h + 1) * half]
        out[h, half : half + 8, 0:half] = line[0:8, h * half : (h + 1) * half]


def gather(mesh, u):
    rows = u.shape[0]
    count, parts = mesh.shape["batch"], mesh.shape["temp"]
    me = lax.axis_index("batch")
    if count != 8 or parts != 4:
        return [(lax.all_gather(u, "batch", axis=0, tiled=True), 0 * me)]

    def send(a, to):
        pairs = []
        for b in range(count):
            for t in range(parts):
                z, y, x, c = b // 2, b % 2, t // 2, t % 2
                z, y, x, c = to(z, y, x, c)
                pairs.append((b * parts + t, (z * 2 + y) * parts + x * 2 + c))
        return lax.ppermute(a, ALL, pairs)

    far = lambda z, y, x, c: (z ^ (2 + x), y, x, c)
    near = lambda z, y, x, c: (z ^ 1, y, x, c)
    over_y = lambda z, y, x, c: (z, 1 - y, x, c)
    over_x = lambda z, y, x, c: (z, y, 1 - x, c)
    x = lax.axis_index("temp") // 2
    mine, other = 4 + 2 * x, 6 - 2 * x
    half = rows // 2
    a = send(u, far)
    n = send(u, near)
    y = send(u, over_y)
    ny = send(n, over_y)
    ay = send(a, over_y)
    ax = send(a, over_x)
    d1 = send(ay[:half], over_x)
    d2 = send(ax[half:], over_y)
    return [
        (u, me * rows),
        (n, (me ^ 2) * rows),
        (y, (me ^ 1) * rows),
        (ny, (me ^ 3) * rows),
        (a, (me ^ mine) * rows),
        (ay, (me ^ mine ^ 1) * rows),
        (ax, (me ^ other) * rows),
        (d1, (me ^ other ^ 1) * rows),
        (d2, (me ^ other ^ 1) * rows + half),
    ]


def shards(mesh, embeddings, spread_code, level_index):
    block, width = embeddings.shape[1:]
    parts = mesh.shape["temp"]
    total = block * mesh.shape["batch"]
    me, part = lax.axis_index("batch"), lax.axis_index("temp")
    core = part % 2
    rows = 2 * block // parts

    swap = [(t, t ^ 1) for t in range(parts)]
    theirs = lax.ppermute(level_index, "temp", swap)
    level = jnp.where(
        core == 0,
        jnp.concatenate([level_index, theirs]),
        jnp.concatenate([theirs, level_index]),
    )
    others = [
        lax.ppermute(level, "temp", [(t, (t + 2 * d) % parts) for t in range(parts)])
        for d in range(1, parts // 2)
    ]
    level = jnp.concatenate([level] + others)

    u = lax.dynamic_index_in_dim(embeddings, core, 0, keepdims=False)
    pieces = gather(mesh, u)
    first = me * block + part // 2 * rows
    places = [first, me * block]
    scalars = jnp.concatenate(
        [jnp.stack(places + [s for _, s in pieces]).astype(jnp.int32), level]
    )
    codes = spread_code[None, :]
    high = 8 * pl.cdiv(parts + 2, 8)
    limit = (24 << 20) if total <= 1024 else (56 << 20)
    params = pltpu.CompilerParams(vmem_limit_bytes=limit)
    smem, vmem = pl.BlockSpec(memory_space=pltpu.SMEM), pl.BlockSpec(memory_space=pltpu.VMEM)

    shapes = [
        jax.ShapeDtypeStruct((high, total), jnp.float32),
        jax.ShapeDtypeStruct((rows, total), jnp.float32),
    ]
    if len(pieces) > 1:
        shapes.append(jax.ShapeDtypeStruct((total, width), jnp.bfloat16))
    stats, strip, *whole = pl.pallas_call(
        functools.partial(stats_kernel, len(pieces), rows),
        out_shape=shapes,
        in_specs=[smem, vmem] + [vmem] * len(pieces),
        out_specs=[vmem] * len(shapes),
        scratch_shapes=[pltpu.VMEM((total, TILE), jnp.float32)],
        compiler_params=params,
    )(scalars, codes, *[a for a, _ in pieces])

    t_stats = lax.ppermute(stats, "temp", swap)
    t_strip = lax.ppermute(strip, "temp", swap)
    half = rows // 2
    out = pl.pallas_call(
        functools.partial(mix_kernel, rows, block),
        out_shape=jax.ShapeDtypeStruct((2, half + 8, width), jnp.float32),
        in_specs=[smem] + [vmem] * 5,
        out_specs=vmem,
        scratch_shapes=[pltpu.VMEM((2, block, high), jnp.float32)],
        compiler_params=params,
    )(
        jnp.concatenate([jnp.stack(places).astype(jnp.int32), level]),
        stats,
        strip,
        t_stats,
        t_strip,
        whole[0] if whole else pieces[0][0],
    )
    back = lax.ppermute(out[0], "temp", [(t + 1, t) for t in range(0, parts, 2)])
    mine = jnp.where(core == 0, back, out[1])
    return mine[:half], mine[half, :half]


def solution(mesh):
    in_specs = (P(None, "batch", None), P(), P("temp"))
    out_specs = (P(("batch", "temp"), None), P(("batch", "temp")))
    return jax.shard_map(
        functools.partial(shards, mesh),
        mesh=mesh,
        in_specs=in_specs,
        out_specs=out_specs,
        check_vma=False,
    )
```

```python
import functools

import jax
import jax.numpy as jnp
from jax import lax
from jax.experimental import pallas as pl
from jax.experimental.pallas import tpu as pltpu
from jax.sharding import PartitionSpec as P

WEIGHT = 16.0
NEG = -1e30
LOG2E = 1.4426950408889634
CODES = 6
TILE = 256
CHUNK = 128
SPAN = 1024
ALL = ("batch", "temp")
SMEM = pl.BlockSpec(memory_space=pltpu.SMEM)
VMEM = pl.BlockSpec(memory_space=pltpu.VMEM)


def carried(count, body, carry):
    if count <= 8:
        for i in range(count):
            carry = body(i, carry)
        return carry
    return lax.fori_loop(0, count, body, carry)


def at(i, size):
    return pl.ds(i * size if isinstance(i, int) else pl.multiple_of(i * size, size), size)


def widths(code, width):
    root = jnp.sqrt(jnp.float32(width))
    return [jnp.exp2(0.5 * (code - jnp.float32(level))) / root for level in range(CODES)]


def powers(d, widest, wide):
    e = [None] * CODES
    e[5], e[4] = jnp.exp2(d * widest), jnp.exp2(d * wide)
    for level in (3, 2, 1, 0):
        e[level] = e[level + 2] * e[level + 2]
    return e


def columns(gram, count, bases):
    size = min(CHUNK, count)
    steps = count // size
    tile = gram.shape[1]
    best = carried(
        steps,
        lambda i, best: jnp.maximum(best, jnp.max(gram[at(i, size), :], axis=0, keepdims=True)),
        jnp.full((1, tile), NEG, jnp.float32),
    )

    def add(i, sums):
        e = powers(gram[at(i, size), :] - best, *bases)
        return tuple(s + jnp.sum(v, axis=0, keepdims=True) for s, v in zip(sums, e))

    return best, carried(steps, add, (jnp.zeros((1, tile), jnp.float32),) * CODES)


def times(a, b):
    return lax.dot_general(a, b, (((1,), (1,)), ((), ())), preferred_element_type=jnp.float32)


def hide_diagonal(gram, rows):
    square = gram[rows, :]
    own = lax.broadcasted_iota(jnp.int32, square.shape, 0) == lax.broadcasted_iota(
        jnp.int32, square.shape, 1
    )
    gram[rows, :] = jnp.where(own, NEG, square)


def bases_of(code, width):
    beta = widths(code.astype(jnp.float32), width)
    return beta[5] * LOG2E, beta[4] * LOG2E


def tiles(total):
    return [(i, min(TILE, total - i)) for i in range(0, total, TILE)]


def first_kernel(place, rows, scalars, codes, *refs):
    *pieces, stats, strip, whole, gram = refs if place else (*refs[:-1], refs[0], refs[-1])
    if place:
        place(scalars, pieces, whole)
    total, width = whole.shape
    mine = pl.ds(pl.multiple_of(scalars[0], rows), rows)

    def tile(cols, size):
        part = gram.at[:, 0:size]
        part[...] = times(whole[...], whole[cols, :])
        hide_diagonal(part, cols)
        strip[:, cols] = part[mine, :]
        best, sums = columns(part, total, bases_of(codes[:, cols], width))
        stats[0:1, cols] = best
        for level in range(CODES):
            stats[1 + level : 2 + level, cols] = sums[level]
        stats[1 + CODES :, cols] = jnp.zeros((stats.shape[0] - 1 - CODES, size), jnp.float32)

    if total <= 4 * TILE:
        for start, size in tiles(total):
            tile(pl.ds(start, size), size)
    else:

        @pl.loop(0, total // TILE)
        def _(i):
            tile(at(i, TILE), TILE)


def place_first(scalars, pieces, whole):
    u, p, q, f, a = pieces
    block, half = u.shape[0], f.shape[0]
    core = scalars[1]
    whole[0:block, :] = u[...]
    whole[pl.ds(pl.multiple_of((2 - core) * block, block), block), :] = p[...]
    whole[pl.ds(pl.multiple_of((1 + core) * block, block), block), :] = q[0:block, :]
    whole[3 * block : 4 * block, :] = q[block : 2 * block, :]
    whole[4 * block : 4 * block + half, :] = f[...]
    whole[4 * block + half : 5 * block, :] = a[...]


def place_second(core, n, a, b, c, whole):
    half = n.shape[0]
    whole[0 : 2 * half, :] = b[0 : 2 * half, :]
    whole[2 * half : 3 * half, :] = n[...]
    spot = lambda i: pl.ds(pl.multiple_of(i * half, half), half)
    whole[spot(3 + core), :] = a[...]
    whole[spot(4 - core), :] = c[0:half, :]
    whole[5 * half : 6 * half, :] = c[half : 2 * half, :]


def second_kernel(
    rows, scalars, codes, early, e_stats, e_strip, b, n, a, c, keep, send, stats, strip, late, gram
):
    core = scalars[1]
    place_second(core, n, a, b, c, late)
    head, width = early.shape
    tail = late.shape[0]
    mine = pl.ds(pl.multiple_of(scalars[0], rows), rows)
    strip[:, 0:head] = e_strip[...]
    for start, size in tiles(tail):
        cols = pl.ds(start, size)
        part = gram.at[:, 0:size]
        part[0:head, :] = times(early[...], late[cols, :])
        part[head : head + tail, :] = times(late[...], late[cols, :])
        hide_diagonal(part, pl.ds(head + start, size))
        strip[:, head + start : head + start + size] = part[mine, :]
        best, sums = columns(
            part, head + tail, bases_of(codes[:, head + start : head + start + size], width)
        )
        stats[0:1, head + start : head + start + size] = best
        for level in range(CODES):
            stats[1 + level : 2 + level, head + start : head + start + size] = sums[level]
    for start, size in tiles(head):
        cols = pl.ds(start, size)
        part = gram.at[0:tail, 0:size]
        part[...] = times(late[...], early[cols, :])
        bases = bases_of(codes[:, cols], width)
        best, sums = columns(part, tail, bases)
        before = e_stats[0:1, cols]
        top = jnp.maximum(best, before)
        was, now = powers(before - top, *bases), powers(best - top, *bases)
        stats[0:1, cols] = top
        for level in range(CODES):
            stats[1 + level : 2 + level, cols] = (
                e_stats[1 + level : 2 + level, cols] * was[level] + sums[level] * now[level]
            )
    line = jnp.zeros((1, head + tail), jnp.float32)
    lane = lax.broadcasted_iota(jnp.int32, line.shape, 1)
    level = scalars[2].astype(jnp.float32)
    theirs = b[2 * n.shape[0] : 2 * n.shape[0] + 1, 0:1].astype(jnp.float32)
    stats[1 + CODES :, :] = jnp.where(lane < 128, level, theirs)
    half = rows // 2
    keep[0:half, :] = strip[pl.ds(pl.multiple_of(core * half, half), half), :]
    send[0:half, :] = strip[pl.ds(pl.multiple_of((1 - core) * half, half), half), :]
    keep[half:, :] = stats[...]
    send[half:, :] = stats[...]


class Mixer:
    def __init__(self, scalars, block, width, codes, keep, recv, turned):
        self.codes, self.width, self.block = codes, width, block
        self.rows = keep.shape[0] - 8
        self.student = scalars[1] == 1
        self.keep, self.recv = keep, recv
        rows, own = self.rows, pl.ds(pl.multiple_of(scalars[3], block), block)
        code = codes[:, own].astype(jnp.float32)
        turned[0] = self.pick(rows, rows + 8, own, True).T
        turned[1] = self.pick(rows, rows + 8, own, False).T
        turned[2] = jnp.broadcast_to(code, (8, block)).T
        mine = pl.ds(pl.multiple_of(scalars[4], rows), rows)
        s, t = turned[0, mine, :], turned[1, mine, :]
        self.beta = widths(turned[2, mine, 0:1], width)
        found = [
            ref[rows + 1 + CODES : rows + 2 + CODES, lane : lane + 1]
            for ref in (keep, recv)
            for lane in (0, 128)
        ]
        self.count = [sum(jnp.where(v == jnp.float32(c), 1.0, 0.0) for v in found) for c in range(CODES)]
        self.s_top, self.t_top = s[:, 0:1], t[:, 0:1]
        self.s_sum = [s[:, 1 + c : 2 + c] for c in range(CODES)]
        self.t_sum = [t[:, 1 + c : 2 + c] for c in range(CODES)]

    def pick(self, low, high, cols, student):
        here, there = self.keep[low:high, cols], self.recv[low:high, cols]
        return jnp.where(self.student == student, here, there)

    def weighted(self, d, beta, sums):
        e = powers(d, beta[5] * LOG2E, beta[4] * LOG2E)
        return sum(v * (n * b / s) for v, n, b, s in zip(e, self.count, beta, sums))

    def part(self, cols):
        rows = self.rows
        gs, gt = self.pick(0, rows, cols, True), self.pick(0, rows, cols, False)
        s, t = self.pick(rows, rows + 8, cols, True), self.pick(rows, rows + 8, cols, False)
        beta = widths(self.codes[:, cols].astype(jnp.float32), self.width)
        lines = lambda a: [a[1 + c : 2 + c] for c in range(CODES)]
        p_row = self.weighted(gt - self.t_top, self.beta, self.t_sum)
        q_row = self.weighted(gs - self.s_top, self.beta, self.s_sum)
        p_col = self.weighted(gt - t[0:1], beta, lines(t))
        q_col = self.weighted(gs - s[0:1], beta, lines(s))
        mix = WEIGHT * ((q_row - p_row) + (q_col - p_col))
        return mix.astype(jnp.bfloat16), jnp.sum(p_row * (gt - gs), axis=1, keepdims=True)

    def store_loss(self, loss, out):
        for c in range(CODES):
            loss = loss + self.count[c] * (
                self.beta[c] * (self.s_top - self.t_top)
                + (jnp.log(self.s_sum[c]) - jnp.log(self.t_sum[c]))
            )
        out[...] = jnp.broadcast_to(loss, (self.rows, 128)).T[0:1, :]


def product(a, b):
    return jnp.dot(a, b, preferred_element_type=jnp.float32)


def mix_kernel(
    scalars, codes, keep, recv, early, their_early, b, n, a, c, their_bc, their_na, out, loss, late, turned
):
    block, half = 2 * n.shape[0], n.shape[0]
    mixer = Mixer(scalars, block, out.shape[1], codes, keep, recv, turned)
    head, tail = early.shape[0], late.shape[0]
    mix_head, loss_head = mixer.part(pl.ds(0, head))
    mix_tail, loss_tail = mixer.part(pl.ds(head, tail))
    mixer.store_loss(loss_head + loss_tail, loss)

    @pl.when(scalars[1] == 1)
    def _():
        place_second(1, n, a, b, c, late)
        out[...] = product(mix_head, early[...]) + product(mix_tail, late[...])

    @pl.when(scalars[1] == 0)
    def _():
        tail_b, tail_c = their_bc.at[0:block, :], their_bc.at[block : 2 * block, :]
        place_second(1, their_na.at[0:half, :], their_na.at[half:block, :], tail_b, tail_c, late)
        out[...] = product(mix_head, their_early[...]) + product(mix_tail, late[...])


def wide_mix_kernel(block, scalars, codes, keep, recv, student, out, loss, turned):
    total, width = student.shape
    mixer = Mixer(scalars, block, width, codes, keep, recv, turned)
    span = min(SPAN, total)

    def step(i, carry):
        mix, gap = mixer.part(at(i, span))
        return carry[0] + product(mix, student[at(i, span), :]), carry[1] + gap

    zero = jnp.zeros((mixer.rows, width), jnp.float32), jnp.zeros((mixer.rows, 1), jnp.float32)
    out[...], gap = lax.fori_loop(0, total // span, step, zero)
    mixer.store_loss(gap, loss)


def call(kernel, shapes, scratch, limit, *args):
    return pl.pallas_call(
        kernel,
        out_shape=shapes,
        in_specs=[SMEM] + [VMEM] * (len(args) - 1),
        out_specs=[VMEM] * len(shapes),
        scratch_shapes=scratch,
        compiler_params=pltpu.CompilerParams(vmem_limit_bytes=limit << 20),
    )(*args)


def shape(*dims, dtype=jnp.float32):
    return jax.ShapeDtypeStruct(dims, dtype)


def shards(mesh, embeddings, spread_code, level_index):
    block, width = embeddings.shape[1:]
    batches, parts = mesh.shape["batch"], mesh.shape["temp"]
    total = block * batches
    me, part = lax.axis_index("batch"), lax.axis_index("temp")
    x, core = part // 2, part % 2
    rows, half = block // 2, block // 4

    def send(a, to):
        pairs = []
        for b in range(batches):
            for t in range(parts):
                there = to(b, t // 2, t % 2)
                pairs.append((b * parts + t, there[0] * parts + there[1] * 2 + there[2]))
        return lax.ppermute(a, ALL, pairs)

    over_core = lambda b, x, c: (b, x, 1 - c)
    over_x = lambda b, x, c: (b, 1 - x, c)
    u = lax.dynamic_index_in_dim(embeddings, core, 0, keepdims=False)
    out_shapes = [shape(half, width), shape(1, half)]

    if batches != 8 or parts != 4:
        whole = lax.all_gather(u, "batch", axis=0, tiled=True)
        theirs = send(level_index, over_x)
        codes = spread_code[None, :]
        scalars = jnp.stack(
            [me * block + x * rows, core, level_index[0], me * block, x * rows + core * half]
        ).astype(jnp.int32)
        stats, strip = call(
            functools.partial(first_kernel, None, rows),
            [shape(8, total), shape(rows, total)],
            [pltpu.VMEM((total, TILE), jnp.float32)],
            56,
            scalars,
            codes,
            whole,
        )
        lane = jnp.arange(total)[None, :]
        line = jnp.where(lane < 128, level_index[0], theirs[0]).astype(jnp.float32)
        stats = jnp.concatenate([stats[: 1 + CODES], line])
        share = lambda c: lax.dynamic_slice_in_dim(strip, c * half, half)
        keep = jnp.concatenate([share(core), stats])
        recv = send(jnp.concatenate([share(1 - core), stats]), over_core)
        student = jnp.where(core == 1, whole, send(whole, over_core))
        out, loss = call(
            functools.partial(wide_mix_kernel, block),
            out_shapes,
            [pltpu.VMEM((3, block, 8), jnp.float32)],
            56,
            scalars,
            codes,
            keep,
            recv,
            student,
        )
        return out, loss[0]

    near = lambda b, x, c: (b ^ 2, x, c)
    far = lambda b, x, c: (b ^ 4, x, c)
    over_y = lambda b, x, c: (b ^ 1, x, c)
    either = lambda even, odd: lambda b, x, c: (odd if c else even)(b, x, c)
    row = lambda a: lax.dynamic_slice_in_dim(a, x * rows, rows, 0)
    f = send(row(u), far)
    p = send(u, either(near, over_y))
    n = send(f, near)
    q = send(jnp.concatenate([u, p]), either(over_y, near))
    fa = send(f, over_y)
    level = jnp.broadcast_to(level_index.astype(jnp.bfloat16), (16, width))
    b = send(jnp.concatenate([f, fa, level]), over_x)
    a = send(n, either(over_x, over_y))
    c = send(jnp.concatenate([n, a]), either(over_y, over_x))

    block_codes = [
        lax.dynamic_slice_in_dim(spread_code, (me ^ m) * block, block) for m in range(batches)
    ]
    first = lambda m: lax.dynamic_slice_in_dim(block_codes[m], x * rows, rows)
    second = lambda m: lax.dynamic_slice_in_dim(block_codes[m], (1 - x) * rows, rows)
    codes = jnp.concatenate(
        block_codes[:4]
        + [first(4), first(5), second(4), second(5), first(6), second(6), first(7), second(7)]
    )[None, :]
    scalars = jnp.stack(
        [x * rows, core, level_index[0], 0 * core, x * rows + core * half]
    ).astype(jnp.int32)
    head = 5 * block
    e_stats, e_strip, early = call(
        functools.partial(first_kernel, place_first, rows),
        [shape(8, head), shape(rows, head), shape(head, width, dtype=jnp.bfloat16)],
        [pltpu.VMEM((head, TILE), jnp.float32)],
        16,
        scalars,
        codes,
        u,
        p,
        q,
        f,
        fa,
    )
    their_early = send(early, over_core)
    their_na = send(jnp.concatenate([n, a]), over_core)
    their_bc = send(jnp.concatenate([b[:block], c]), over_core)
    tail = total - head
    keep, mail = call(
        functools.partial(second_kernel, rows),
        [shape(half + 8, total), shape(half + 8, total)],
        [
            pltpu.VMEM((8, total), jnp.float32),
            pltpu.VMEM((rows, total), jnp.float32),
            pltpu.VMEM((tail, width), jnp.bfloat16),
            pltpu.VMEM((total, TILE), jnp.float32),
        ],
        16,
        scalars,
        codes,
        early,
        e_stats,
        e_strip,
        b,
        n,
        a,
        c,
    )
    recv = send(mail, over_core)
    out, loss = call(
        mix_kernel,
        out_shapes,
        [pltpu.VMEM((tail, width), jnp.bfloat16), pltpu.VMEM((3, block, 8), jnp.float32)],
        16,
        scalars,
        codes,
        keep,
        recv,
        early,
        their_early,
        b,
        n,
        a,
        c,
        their_bc,
        their_na,
    )
    return out, loss[0]


def solution(mesh):
    in_specs = (P(None, "batch", None), P(), P("temp"))
    out_specs = (P(("batch", "temp"), None), P(("batch", "temp")))
    return jax.shard_map(
        functools.partial(shards, mesh),
        mesh=mesh,
        in_specs=in_specs,
        out_specs=out_specs,
        check_vma=False,
    )
```

```python
import functools

import jax
import jax.numpy as jnp
from jax import lax
from jax.experimental import pallas as pl
from jax.experimental.pallas import tpu as pltpu
from jax.sharding import PartitionSpec as P

WEIGHT = 16.0
NEG = -1e30
LOG2E = 1.4426950408889634
CODES = 6
TILE = 256
CHUNK = 128
SPAN = 1024
ALL = ("batch", "temp")
SMEM = pl.BlockSpec(memory_space=pltpu.SMEM)
VMEM = pl.BlockSpec(memory_space=pltpu.VMEM)


def carried(count, body, carry):
    if count <= 8:
        for i in range(count):
            carry = body(i, carry)
        return carry
    return lax.fori_loop(0, count, body, carry)


def at(i, size):
    return pl.ds(i * size if isinstance(i, int) else pl.multiple_of(i * size, size), size)


def widths(code, width):
    root = jnp.sqrt(jnp.float32(width))
    return [jnp.exp2(0.5 * (code - jnp.float32(level))) / root for level in range(CODES)]


def powers(d, widest, wide):
    e = [None] * CODES
    e[5], e[4] = jnp.exp2(d * widest), jnp.exp2(d * wide)
    for level in (3, 2, 1, 0):
        e[level] = e[level + 2] * e[level + 2]
    return e


def columns(gram, count, bases):
    size = min(CHUNK, count)
    steps = count // size
    tile = gram.shape[1]
    best = carried(
        steps,
        lambda i, best: jnp.maximum(best, jnp.max(gram[at(i, size), :], axis=0, keepdims=True)),
        jnp.full((1, tile), NEG, jnp.float32),
    )

    def add(i, sums):
        e = powers(gram[at(i, size), :] - best, *bases)
        return tuple(s + jnp.sum(v, axis=0, keepdims=True) for s, v in zip(sums, e))

    return best, carried(steps, add, (jnp.zeros((1, tile), jnp.float32),) * CODES)


def times(a, b):
    return lax.dot_general(a, b, (((1,), (1,)), ((), ())), preferred_element_type=jnp.float32)


def hide_diagonal(gram, rows):
    square = gram[rows, :]
    own = lax.broadcasted_iota(jnp.int32, square.shape, 0) == lax.broadcasted_iota(
        jnp.int32, square.shape, 1
    )
    gram[rows, :] = jnp.where(own, NEG, square)


def bases_of(code, width):
    beta = widths(code.astype(jnp.float32), width)
    return beta[5] * LOG2E, beta[4] * LOG2E


def tiles(total):
    return [(i, min(TILE, total - i)) for i in range(0, total, TILE)]


def position():
    part = lax.axis_index("temp")
    return lax.axis_index("batch"), part // 2, part % 2


def spot(i, size):
    return pl.ds(pl.multiple_of(i * size, size), size)


def order_codes(spread, line, block):
    me, x, core = position()
    half = block // 2
    cut = [spread[:, spot(me ^ m, block)] for m in range(8)]
    cut[4:] = [jnp.where(x == 0, v, pltpu.roll(v, half, 1)) for v in cut[4:]]
    left = lax.broadcasted_iota(jnp.int32, cut[0].shape, 1) < half
    other = [None] * 4 + [pltpu.roll(v, half, 1) for v in cut[4:]]
    even = core == 0
    order = cut[:3] + [
        jnp.where(left, cut[4], other[6]),
        cut[3],
        jnp.where(left, other[4], other[5]),
        jnp.where(left, other[5], jnp.where(even, cut[6], other[7])),
        jnp.where(left, jnp.where(even, cut[7], other[6]), cut[7]),
    ]
    for m, v in enumerate(order):
        line[:, m * block : (m + 1) * block] = v


def first_kernel(staged, spread, *refs):
    me, x, core = position()
    if staged:
        *pieces, codes, stats, strip, whole, gram = refs
        block = pieces[0].shape[0]
        order_codes(spread, codes, block)
        row = 0
        for piece in pieces:
            whole[row : row + piece.shape[0], :] = piece[...]
            row += piece.shape[0]
        first_row = x * (block // 2)
    else:
        whole, stats, strip, gram = refs
        codes, block = spread, strip.shape[0] * 2
        first_row = me * block + x * (block // 2)
    total, width = whole.shape
    mine = pl.ds(pl.multiple_of(first_row, block // 2), block // 2)

    def tile(cols, size):
        part = gram.at[:, 0:size]
        part[...] = times(whole[...], whole[cols, :])
        hide_diagonal(part, cols)
        strip[:, cols] = part[mine, :]
        best, sums = columns(part, total, bases_of(codes[:, cols], width))
        stats[0:1, cols] = best
        for level in range(CODES):
            stats[1 + level : 2 + level, cols] = sums[level]
        stats[1 + CODES :, cols] = jnp.zeros((stats.shape[0] - 1 - CODES, size), jnp.float32)

    if total <= 4 * TILE:
        for start, size in tiles(total):
            tile(pl.ds(start, size), size)
    else:

        @pl.loop(0, total // TILE)
        def _(i):
            tile(at(i, TILE), TILE)


def swapped(a, block):
    left, right = a[:, -2 * block : -block], a[:, -block:]
    half = block // 2
    low = lax.broadcasted_iota(jnp.int32, left.shape, 1) < half
    return jnp.where(low, left, pltpu.roll(right, half, 1)), jnp.where(
        low, pltpu.roll(left, half, 1), right
    )


def add_rows(x, codes, early, late, before, stats, strip, gram):
    head, width = early.shape
    tail = late.shape[0]
    for start, size in tiles(tail):
        cols, lines = pl.ds(start, size), slice(head + start, head + start + size)
        part = gram.at[0 : head + tail, 0:size]
        part[0:head, :] = times(early[...], late[cols, :])
        part[head : head + tail, :] = times(late[...], late[cols, :])
        hide_diagonal(part, pl.ds(head + start, size))
        strip[:, lines] = part[spot(x, strip.shape[0]), :]
        best, sums = columns(part, head + tail, bases_of(codes[:, lines], width))
        stats[0:1, lines] = best
        for level in range(CODES):
            stats[1 + level : 2 + level, lines] = sums[level]
    for start, size in tiles(head):
        cols = pl.ds(start, size)
        part = gram.at[0:tail, 0:size]
        part[...] = times(late[...], early[cols, :])
        bases = bases_of(codes[:, cols], width)
        best, sums = columns(part, tail, bases)
        top = jnp.maximum(best, before[0:1, cols])
        was, now = powers(before[0:1, cols] - top, *bases), powers(best - top, *bases)
        stats[0:1, cols] = top
        for level in range(CODES):
            stats[1 + level : 2 + level, cols] = (
                before[1 + level : 2 + level, cols] * was[level] + sums[level] * now[level]
            )


def second_kernel(codes, early, before, part_strip, ny, fa, fb, ga, stats, strip, whole, gram):
    _, x, core = position()
    head, block = early.shape[0], ny.shape[0]
    half = block // 2
    late = whole.at[head:, :]
    late[0:block, :] = ny[...]
    late[spot(2 + core, half), :] = fa[0:half, :]
    late[spot(3 - core, half), :] = fb[0:half, :]
    late[4 * half : 5 * half, :] = fb[half : 2 * half, :]
    late[5 * half : 6 * half, :] = ga[...]
    whole[0:head, :] = early[...]
    strip[:, 0:head] = part_strip[...]
    add_rows(x, codes, early, late, before, stats, strip, gram)
    stats[1 + CODES :, :] = jnp.zeros((stats.shape[0] - 1 - CODES, stats.shape[1]), jnp.float32)


def third_kernel(
    codes, early, before, part_strip, level_index, fa, fb, late, keep, send, stats, strip, gram
):
    _, x, core = position()
    head, block = early.shape[0], late.shape[0]
    half = block // 4
    strip[:, 0:head] = part_strip[...]
    add_rows(x, codes, early, late, before, stats, strip, gram)
    lane = lax.broadcasted_iota(jnp.int32, (1, stats.shape[1]), 1)
    level = level_index[0].astype(jnp.float32)
    theirs = jnp.where(core == 0, fa[block // 2 : block // 2 + 1, 0:1], fb[block : block + 1, 0:1])
    stats[1 + CODES :, :] = jnp.where(lane < 128, level, theirs.astype(jnp.float32))
    keep[0:half, :] = strip[spot(core, half), :]
    send[0:half, :] = strip[spot(1 - core, half), :]
    keep[half:, :] = stats[...]
    send[half:, :] = stats[...]
    left, right = swapped(send[:, -2 * block :], block)
    send[:, -2 * block : -block] = left
    send[:, -block:] = right


class Mixer:
    def __init__(self, own, width, codes, keep, recv, turned):
        _, x, core = position()
        self.codes, self.width = codes, width
        self.rows = rows = keep.shape[0] - 8
        self.student = core == 1
        self.keep, self.recv = keep, recv
        block = 4 * rows
        own = spot(own, block)
        code = codes[:, own].astype(jnp.float32)
        turned[0] = self.pick(rows, rows + 8, own, True).T
        turned[1] = self.pick(rows, rows + 8, own, False).T
        turned[2] = jnp.broadcast_to(code, (8, block)).T
        mine = spot(2 * x + core, rows)
        s, t = turned[0, mine, :], turned[1, mine, :]
        self.beta = widths(turned[2, mine, 0:1], width)
        found = [
            ref[rows + 1 + CODES : rows + 2 + CODES, lane : lane + 1]
            for ref in (keep, recv)
            for lane in (0, 128)
        ]
        self.count = [sum(jnp.where(v == jnp.float32(c), 1.0, 0.0) for v in found) for c in range(CODES)]
        self.s_top, self.t_top = s[:, 0:1], t[:, 0:1]
        self.s_sum = [s[:, 1 + c : 2 + c] for c in range(CODES)]
        self.t_sum = [t[:, 1 + c : 2 + c] for c in range(CODES)]

    def pick(self, low, high, cols, student):
        here, there = self.keep[low:high, cols], self.recv[low:high, cols]
        return jnp.where(self.student == student, here, there)

    def weighted(self, d, beta, sums):
        e = powers(d, beta[5] * LOG2E, beta[4] * LOG2E)
        return sum(v * (n * b / s) for v, n, b, s in zip(e, self.count, beta, sums))

    def part(self, cols):
        rows = self.rows
        gs, gt = self.pick(0, rows, cols, True), self.pick(0, rows, cols, False)
        s, t = self.pick(rows, rows + 8, cols, True), self.pick(rows, rows + 8, cols, False)
        beta = widths(self.codes[:, cols].astype(jnp.float32), self.width)
        lines = lambda a: [a[1 + c : 2 + c] for c in range(CODES)]
        p_row = self.weighted(gt - self.t_top, self.beta, self.t_sum)
        q_row = self.weighted(gs - self.s_top, self.beta, self.s_sum)
        p_col = self.weighted(gt - t[0:1], beta, lines(t))
        q_col = self.weighted(gs - s[0:1], beta, lines(s))
        mix = WEIGHT * ((q_row - p_row) + (q_col - p_col))
        return mix.astype(jnp.bfloat16), jnp.sum(p_row * (gt - gs), axis=1, keepdims=True)

    def store_loss(self, loss, out):
        for c in range(CODES):
            loss = loss + self.count[c] * (
                self.beta[c] * (self.s_top - self.t_top)
                + (jnp.log(self.s_sum[c]) - jnp.log(self.t_sum[c]))
            )
        out[...] = jnp.broadcast_to(loss, (self.rows, 128)).T[0:1, :]


def product(a, b):
    return jnp.dot(a, b, preferred_element_type=jnp.float32)


def mix_kernel(codes, keep, recv, early, late, sooner, later, out, loss, turned, whole):
    mixer = Mixer(0, out.shape[1], codes, keep, recv, turned)
    head, total = early.shape[0], codes.shape[1]
    mix, gap = mixer.part(pl.ds(0, total))
    mixer.store_loss(gap, loss)

    @pl.when(mixer.student)
    def _():
        out[...] = product(mix[:, :head], early[...]) + product(mix[:, head:], late[...])

    @pl.when(jnp.logical_not(mixer.student))
    def _():
        half = late.shape[0] // 2
        for there, places in (
            (sooner, (0, 1, 4, 5, 2, 3, 6, 11, 7)),
            (later, (8, 9, 10, 12, 14, 13, 15)),
        ):
            for i, place in enumerate(places):
                whole[place * half : (place + 1) * half, :] = there[i * half : (i + 1) * half, :]
        out[...] = product(mix, whole[...])


def wide_mix_kernel(codes, keep, recv, student, out, loss, turned):
    total, width = student.shape
    mixer = Mixer(lax.axis_index("batch"), width, codes, keep, recv, turned)
    span = min(SPAN, total)

    def step(i, carry):
        mix, gap = mixer.part(at(i, span))
        return carry[0] + product(mix, student[at(i, span), :]), carry[1] + gap

    zero = jnp.zeros((mixer.rows, width), jnp.float32), jnp.zeros((mixer.rows, 1), jnp.float32)
    out[...], gap = lax.fori_loop(0, total // span, step, zero)
    mixer.store_loss(gap, loss)


def call(kernel, shapes, scratch, limit, *args):
    return pl.pallas_call(
        kernel,
        out_shape=shapes,
        in_specs=[SMEM if a.shape == (1,) else VMEM for a in args],
        out_specs=[VMEM] * len(shapes),
        scratch_shapes=scratch,
        compiler_params=pltpu.CompilerParams(vmem_limit_bytes=limit << 20),
    )(*args)


def join(parts, *behind):
    def kernel(*refs):
        row = 0
        for part in refs[: len(parts)]:
            refs[-1][row : row + part.shape[0], :] = part[...]
            row += part.shape[0]

    dims = sum(p.shape[0] for p in parts), parts[0].shape[1]
    return call(kernel, [shape(*dims, dtype=parts[0].dtype)], [], 16, *parts, *behind)[0]


def shape(*dims, dtype=jnp.float32):
    return jax.ShapeDtypeStruct(dims, dtype)


def shards(mesh, embeddings, spread_code, level_index):
    block, width = embeddings.shape[1:]
    batches, parts = mesh.shape["batch"], mesh.shape["temp"]
    total = block * batches
    me, part = lax.axis_index("batch"), lax.axis_index("temp")
    x, core = part // 2, part % 2
    rows, half = block // 2, block // 4

    def send(a, to):
        pairs = []
        for b in range(batches):
            for t in range(parts):
                there = to(b, t // 2, t % 2)
                pairs.append((b * parts + t, there[0] * parts + there[1] * 2 + there[2]))
        return lax.ppermute(a, ALL, pairs)

    over_core = lambda b, x, c: (b, x, 1 - c)
    over_x = lambda b, x, c: (b, 1 - x, c)
    u = lax.dynamic_index_in_dim(embeddings, core, 0, keepdims=False)
    out_shapes = [shape(half, width), shape(1, half)]
    codes = spread_code[None, :]

    if batches != 8 or parts != 4:
        whole = lax.all_gather(u, "batch", axis=0, tiled=True)
        theirs = send(level_index, over_x)
        stats, strip = call(
            functools.partial(first_kernel, False),
            [shape(8, total), shape(rows, total)],
            [pltpu.VMEM((total, TILE), jnp.float32)],
            56,
            codes,
            whole,
        )
        lane = jnp.arange(total)[None, :]
        line = jnp.where(lane < 128, level_index[0], theirs[0]).astype(jnp.float32)
        stats = jnp.concatenate([stats[: 1 + CODES], line])
        share = lambda c: lax.dynamic_slice_in_dim(strip, c * half, half)
        keep = jnp.concatenate([share(core), stats])
        recv = send(jnp.concatenate([share(1 - core), stats]), over_core)
        student = jnp.where(core == 1, whole, send(whole, over_core))
        out, loss = call(
            wide_mix_kernel,
            out_shapes,
            [pltpu.VMEM((3, block, 8), jnp.float32)],
            56,
            codes,
            keep,
            recv,
            student,
        )
        return out, loss[0]

    near = lambda b, x, c: (b ^ 2, x, c)
    far = lambda b, x, c: (b ^ 4, x, c)
    over_y = lambda b, x, c: (b ^ 1, x, c)
    turn = lambda b, x, c: (over_y if c else over_x)(b, x, c)
    return_turn = lambda b, x, c: (over_x if c else over_y)(b, x, c)
    level = jnp.broadcast_to(level_index.astype(jnp.bfloat16), (16, width))
    f = send(lax.dynamic_slice_in_dim(u, x * rows, rows, 0), far)
    n = send(u, near)
    y = send(u, over_y)
    g = send(f, near)
    ny = send(join([y], g), near)
    fa = send(join([f, level]), turn)
    fb = send(join([f, fa[:rows], level], g), return_turn)
    ga = send(g, turn)
    sooner = send(join([u, n, y, f, fa[:rows], g]), over_core)
    some, head = 4 * block, total - block
    codes, a_stats, a_strip, a_rows = call(
        functools.partial(first_kernel, True),
        [
            shape(1, total, dtype=jnp.int32),
            shape(8, some),
            shape(rows, some),
            shape(some, width, dtype=jnp.bfloat16),
        ],
        [pltpu.VMEM((some, TILE), jnp.float32)],
        16,
        codes,
        u,
        y,
        n,
        f,
        g,
    )
    gb = send(join([g, ga], sooner, a_stats), return_turn)
    b_stats, b_strip, b_rows = call(
        second_kernel,
        [shape(8, head), shape(rows, head), shape(head, width, dtype=jnp.bfloat16)],
        [pltpu.VMEM((head, TILE), jnp.float32)],
        16,
        codes,
        a_rows,
        a_stats,
        a_strip,
        ny,
        fa,
        fb,
        ga,
    )
    later = send(join([ny, fb[:block], ga, gb], b_stats), over_core)
    keep, mail = call(
        third_kernel,
        [shape(half + 8, total), shape(half + 8, total)],
        [
            pltpu.VMEM((8, total), jnp.float32),
            pltpu.VMEM((rows, total), jnp.float32),
            pltpu.VMEM((total, TILE), jnp.float32),
        ],
        16,
        codes,
        b_rows,
        b_stats,
        b_strip,
        level_index,
        fa,
        fb,
        gb,
    )
    recv = send(mail, over_core)
    out, loss = call(
        mix_kernel,
        out_shapes,
        [pltpu.VMEM((3, block, 8), jnp.float32), pltpu.VMEM((total, width), jnp.bfloat16)],
        16,
        codes,
        keep,
        recv,
        b_rows,
        gb,
        sooner,
        later,
    )
    return out, loss[0]


def solution(mesh):
    in_specs = (P(None, "batch", None), P(), P("temp"))
    out_specs = (P(("batch", "temp"), None), P(("batch", "temp")))
    return jax.shard_map(
        functools.partial(shards, mesh),
        mesh=mesh,
        in_specs=in_specs,
        out_specs=out_specs,
        check_vma=False,
    )
```

```python
import functools

import jax
import jax.numpy as jnp
from jax import lax
from jax.experimental import pallas as pl
from jax.experimental.pallas import tpu as pltpu
from jax.sharding import PartitionSpec as P

WEIGHT = 16.0
NEG = -1e30
LOG2E = 1.4426950408889634
CODES = 6
TILE = 256
CHUNK = 128
SPAN = 1024
ALL = ("batch", "temp")
SMEM = pl.BlockSpec(memory_space=pltpu.SMEM)
VMEM = pl.BlockSpec(memory_space=pltpu.VMEM)


def carried(count, body, carry):
    if count <= 8:
        for i in range(count):
            carry = body(i, carry)
        return carry
    return lax.fori_loop(0, count, body, carry)


def at(i, size):
    return pl.ds(i * size if isinstance(i, int) else pl.multiple_of(i * size, size), size)


def widths(code, width):
    root = jnp.sqrt(jnp.float32(width))
    return [jnp.exp2(0.5 * (code - jnp.float32(level))) / root for level in range(CODES)]


def powers(d, widest, wide):
    e = [None] * CODES
    e[5], e[4] = jnp.exp2(d * widest), jnp.exp2(d * wide)
    for level in (3, 2, 1, 0):
        e[level] = e[level + 2] * e[level + 2]
    return e


def columns(gram, count, bases):
    size = min(CHUNK, count)
    steps = count // size
    tile = gram.shape[1]
    best = carried(
        steps,
        lambda i, best: jnp.maximum(best, jnp.max(gram[at(i, size), :], axis=0, keepdims=True)),
        jnp.full((1, tile), NEG, jnp.float32),
    )

    def add(i, sums):
        e = powers(gram[at(i, size), :] - best, *bases)
        return tuple(s + jnp.sum(v, axis=0, keepdims=True) for s, v in zip(sums, e))

    return best, carried(steps, add, (jnp.zeros((1, tile), jnp.float32),) * CODES)


def times(a, b):
    return lax.dot_general(a, b, (((1,), (1,)), ((), ())), preferred_element_type=jnp.float32)


def hide_diagonal(gram, rows):
    square = gram[rows, :]
    own = lax.broadcasted_iota(jnp.int32, square.shape, 0) == lax.broadcasted_iota(
        jnp.int32, square.shape, 1
    )
    gram[rows, :] = jnp.where(own, NEG, square)


def bases_of(code, width):
    beta = widths(code.astype(jnp.float32), width)
    return beta[5] * LOG2E, beta[4] * LOG2E


def tiles(total):
    return [(i, min(TILE, total - i)) for i in range(0, total, TILE)]


def position():
    part = lax.axis_index("temp")
    return lax.axis_index("batch"), part // 2, part % 2


def spot(i, size):
    return pl.ds(pl.multiple_of(i * size, size), size)


def order_codes(spread, line, block):
    me, x, core = position()
    half = block // 2
    cut = [spread[:, spot(me ^ m, block)] for m in range(8)]
    cut[4:] = [jnp.where(x == 0, v, pltpu.roll(v, half, 1)) for v in cut[4:]]
    left = lax.broadcasted_iota(jnp.int32, cut[0].shape, 1) < half
    other = [None] * 4 + [pltpu.roll(v, half, 1) for v in cut[4:]]
    even = core == 0
    order = cut[:3] + [
        jnp.where(left, cut[4], other[6]),
        jnp.where(left, other[4], other[5]),
        jnp.where(left, other[5], jnp.where(even, cut[6], other[7])),
        cut[3],
        jnp.where(left, jnp.where(even, cut[7], other[6]), cut[7]),
    ]
    for m, v in enumerate(order):
        line[:, m * block : (m + 1) * block] = v


def first_kernel(staged, spread, *refs):
    me, x, core = position()
    if staged:
        *pieces, codes, stats, strip, whole, gram = refs
        block = pieces[0].shape[0]
        order_codes(spread, codes, block)
        row = 0
        for piece in pieces:
            whole[row : row + piece.shape[0], :] = piece[...]
            row += piece.shape[0]
        first_row = x * (block // 2)
    else:
        whole, stats, strip, gram = refs
        codes, block = spread, strip.shape[0] * 2
        first_row = me * block + x * (block // 2)
    total, width = whole.shape
    mine = pl.ds(pl.multiple_of(first_row, block // 2), block // 2)

    def tile(cols, size, slot=0):
        part = gram.at[slot, :, 0:size]
        part[...] = times(whole[...], whole[cols, :])
        hide_diagonal(part, cols)
        strip[:, cols] = part[mine, :]
        best, sums = columns(part, total, bases_of(codes[:, cols], width))
        stats[0:1, cols] = best
        for level in range(CODES):
            stats[1 + level : 2 + level, cols] = sums[level]
        stats[1 + CODES :, cols] = jnp.zeros((stats.shape[0] - 1 - CODES, size), jnp.float32)

    if staged:
        for slot, (start, size) in enumerate(tiles(total)):
            tile(pl.ds(start, size), size, slot)
    else:

        @pl.loop(0, total // TILE)
        def _(i):
            tile(at(i, TILE), TILE)


def swapped(a, block):
    left, right = a[:, -3 * block : -2 * block], a[:, -block:]
    half = block // 2
    low = lax.broadcasted_iota(jnp.int32, left.shape, 1) < half
    return jnp.where(low, left, pltpu.roll(right, half, 1)), jnp.where(
        low, pltpu.roll(left, half, 1), right
    )


def slots(rows, cols):
    return pltpu.VMEM((len(tiles(cols)), rows, min(cols, TILE)), jnp.float32)


def add_rows(x, codes, early, late, before, stats, strip, gram, wide):
    head, width = early.shape
    tail = late.shape[0]
    for slot, (start, size) in enumerate(tiles(tail)):
        cols, lines = pl.ds(start, size), slice(head + start, head + start + size)
        part = gram.at[slot, :, 0:size]
        part[0:head, :] = times(early[...], late[cols, :])
        part[head : head + tail, :] = times(late[...], late[cols, :])
        hide_diagonal(part, pl.ds(head + start, size))
        strip[:, lines] = part[spot(x, strip.shape[0]), :]
        best, sums = columns(part, head + tail, bases_of(codes[:, lines], width))
        stats[0:1, lines] = best
        for level in range(CODES):
            stats[1 + level : 2 + level, lines] = sums[level]
    for slot, (start, size) in enumerate(tiles(head)):
        cols = pl.ds(start, size)
        part = wide.at[slot, :, 0:size]
        part[...] = times(late[...], early[cols, :])
        bases = bases_of(codes[:, cols], width)
        best, sums = columns(part, tail, bases)
        top = jnp.maximum(best, before[0:1, cols])
        was, now = powers(before[0:1, cols] - top, *bases), powers(best - top, *bases)
        stats[0:1, cols] = top
        for level in range(CODES):
            stats[1 + level : 2 + level, cols] = (
                before[1 + level : 2 + level, cols] * was[level] + sums[level] * now[level]
            )


def second_kernel(codes, early, before, part_strip, fa, fb, ga, stats, strip, whole, gram, wide):
    _, x, core = position()
    head, half = early.shape[0], ga.shape[0]
    late = whole.at[head:, :]
    late[spot(core, half), :] = fa[0:half, :]
    late[spot(1 - core, half), :] = fb[0:half, :]
    late[2 * half : 3 * half, :] = fb[half : 2 * half, :]
    late[3 * half : 4 * half, :] = ga[...]
    whole[0:head, :] = early[...]
    strip[:, 0:head] = part_strip[...]
    add_rows(x, codes, early, late, before, stats, strip, gram, wide)
    stats[1 + CODES :, :] = jnp.zeros((stats.shape[0] - 1 - CODES, stats.shape[1]), jnp.float32)


def third_kernel(codes, early, before, part_strip, late, stats, strip, gram, wide):
    _, x, _ = position()
    strip[:, 0 : early.shape[0]] = part_strip[...]
    add_rows(x, codes, early, late, before, stats, strip, gram, wide)
    stats[1 + CODES :, :] = jnp.zeros((stats.shape[0] - 1 - CODES, stats.shape[1]), jnp.float32)


def last_kernel(
    codes, early, middle, before, strip, level_index, fa, fb, late, keep, send, wide, square
):
    _, x, core = position()
    block, width = late.shape
    half = block // 4
    head = before.shape[1]
    last = slice(head, head + block)
    wide[:, 0 : early.shape[0]] = times(late[...], early[...])
    wide[:, early.shape[0] : head] = times(late[...], middle[...])
    gram = times(late[...], late[...])
    lines, lanes = (lax.broadcasted_iota(jnp.int32, gram.shape, axis) for axis in (0, 1))
    wide[:, last] = jnp.where(lines == lanes, NEG, gram)
    square[...] = jnp.broadcast_to(codes[:, last], (8, block)).astype(jnp.float32).T
    bases = bases_of(square[:, 0:1], width)
    best = jnp.max(wide[...], axis=1, keepdims=True)
    part = powers(wide[...] - best, *bases)
    square[:, 0:1] = best
    for level in range(CODES):
        square[:, 1 + level : 2 + level] = jnp.sum(part[level], axis=1, keepdims=True)
    keep[half:, last] = square[...].T
    for start, size in tiles(head):
        cols = pl.ds(start, size)
        bases = bases_of(codes[:, cols], width)
        best, sums = columns(wide.at[:, cols], block, bases)
        top = jnp.maximum(best, before[0:1, cols])
        was, now = powers(before[0:1, cols] - top, *bases), powers(best - top, *bases)
        keep[half : half + 1, cols] = top
        for level in range(CODES):
            keep[half + 1 + level : half + 2 + level, cols] = (
                before[1 + level : 2 + level, cols] * was[level] + sums[level] * now[level]
            )
    lane = lax.broadcasted_iota(jnp.int32, (1, head + block), 1)
    level = level_index[0].astype(jnp.float32)
    theirs = jnp.where(core == 0, fa[block // 2 : block // 2 + 1, 0:1], fb[block : block + 1, 0:1])
    keep[half + 1 + CODES :, :] = jnp.where(lane < 128, level, theirs.astype(jnp.float32))
    square_t = wide[:, 0:block].T
    for ref, share in ((keep, core), (send, 1 - core)):
        ref[0:half, 0:head] = strip[spot(share, half), :]
        here = jnp.where(share == 0, square_t[0:half], square_t[half : 2 * half])
        there = jnp.where(
            share == 0, square_t[2 * half : 3 * half], square_t[3 * half : 4 * half]
        )
        ref[0:half, last] = jnp.where(x == 0, here, there)
    send[half:, :] = keep[half:, :]
    left, right = swapped(send, block)
    send[:, -3 * block : -2 * block] = left
    send[:, -block:] = right


class Mixer:
    def __init__(self, own, width, codes, keep, recv, turned):
        _, x, core = position()
        self.codes, self.width = codes, width
        self.rows = rows = keep.shape[0] - 8
        self.student = core == 1
        self.keep, self.recv = keep, recv
        block = 4 * rows
        own = spot(own, block)
        code = codes[:, own].astype(jnp.float32)
        turned[0] = self.pick(rows, rows + 8, own, True).T
        turned[1] = self.pick(rows, rows + 8, own, False).T
        turned[2] = jnp.broadcast_to(code, (8, block)).T
        mine = spot(2 * x + core, rows)
        s, t = turned[0, mine, :], turned[1, mine, :]
        self.beta = widths(turned[2, mine, 0:1], width)
        found = [
            ref[rows + 1 + CODES : rows + 2 + CODES, lane : lane + 1]
            for ref in (keep, recv)
            for lane in (0, 128)
        ]
        self.count = [sum(jnp.where(v == jnp.float32(c), 1.0, 0.0) for v in found) for c in range(CODES)]
        self.s_top, self.t_top = s[:, 0:1], t[:, 0:1]
        self.s_sum = [s[:, 1 + c : 2 + c] for c in range(CODES)]
        self.t_sum = [t[:, 1 + c : 2 + c] for c in range(CODES)]

    def pick(self, low, high, cols, student):
        here, there = self.keep[low:high, cols], self.recv[low:high, cols]
        return jnp.where(self.student == student, here, there)

    def weighted(self, d, beta, sums):
        e = powers(d, beta[5] * LOG2E, beta[4] * LOG2E)
        return sum(v * (n * b / s) for v, n, b, s in zip(e, self.count, beta, sums))

    def part(self, cols):
        rows = self.rows
        gs, gt = self.pick(0, rows, cols, True), self.pick(0, rows, cols, False)
        s, t = self.pick(rows, rows + 8, cols, True), self.pick(rows, rows + 8, cols, False)
        beta = widths(self.codes[:, cols].astype(jnp.float32), self.width)
        lines = lambda a: [a[1 + c : 2 + c] for c in range(CODES)]
        p_row = self.weighted(gt - self.t_top, self.beta, self.t_sum)
        q_row = self.weighted(gs - self.s_top, self.beta, self.s_sum)
        p_col = self.weighted(gt - t[0:1], beta, lines(t))
        q_col = self.weighted(gs - s[0:1], beta, lines(s))
        mix = WEIGHT * ((q_row - p_row) + (q_col - p_col))
        return mix.astype(jnp.bfloat16), jnp.sum(p_row * (gt - gs), axis=1, keepdims=True)

    def store_loss(self, loss, out):
        for c in range(CODES):
            loss = loss + self.count[c] * (
                self.beta[c] * (self.s_top - self.t_top)
                + (jnp.log(self.s_sum[c]) - jnp.log(self.t_sum[c]))
            )
        out[...] = jnp.broadcast_to(loss, (self.rows, 128)).T[0:1, :]


def product(a, b):
    return jnp.dot(a, b, preferred_element_type=jnp.float32)


def mix_kernel(codes, keep, recv, early, middle, late, sooner, later, out, loss, turned):
    mixer = Mixer(0, out.shape[1], codes, keep, recv, turned)
    mix, gap = mixer.part(pl.ds(0, codes.shape[1]))
    mixer.store_loss(gap, loss)

    def against(*parts):
        row, total = 0, None
        for part in parts:
            term = product(mix[:, row : row + part.shape[0]], part[...])
            row, total = row + part.shape[0], term if total is None else total + term
        out[...] = total

    @pl.when(mixer.student)
    def _():
        against(early, middle, late)

    @pl.when(jnp.logical_not(mixer.student))
    def _():
        against(sooner, later)


def wide_mix_kernel(codes, keep, recv, student, out, loss, turned):
    total, width = student.shape
    mixer = Mixer(lax.axis_index("batch"), width, codes, keep, recv, turned)
    span = min(SPAN, total)

    def step(i, carry):
        mix, gap = mixer.part(at(i, span))
        return carry[0] + product(mix, student[at(i, span), :]), carry[1] + gap

    zero = jnp.zeros((mixer.rows, width), jnp.float32), jnp.zeros((mixer.rows, 1), jnp.float32)
    out[...], gap = lax.fori_loop(0, total // span, step, zero)
    mixer.store_loss(gap, loss)


def call(kernel, shapes, scratch, limit, *args):
    return pl.pallas_call(
        kernel,
        out_shape=shapes,
        in_specs=[SMEM if a.shape == (1,) else VMEM for a in args],
        out_specs=[VMEM] * len(shapes),
        scratch_shapes=scratch,
        compiler_params=pltpu.CompilerParams(vmem_limit_bytes=limit << 20),
    )(*args)


def join(parts, *behind):
    def kernel(*refs):
        row = 0
        for part in refs[: len(parts)]:
            refs[-1][row : row + part.shape[0], :] = part[...]
            row += part.shape[0]

    dims = sum(p.shape[0] for p in parts), parts[0].shape[1]
    return call(kernel, [shape(*dims, dtype=parts[0].dtype)], [], 16, *parts, *behind)[0]


def shape(*dims, dtype=jnp.float32):
    return jax.ShapeDtypeStruct(dims, dtype)


def shards(mesh, embeddings, spread_code, level_index):
    block, width = embeddings.shape[1:]
    batches, parts = mesh.shape["batch"], mesh.shape["temp"]
    total = block * batches
    me, part = lax.axis_index("batch"), lax.axis_index("temp")
    x, core = part // 2, part % 2
    rows, half = block // 2, block // 4

    def send(a, to):
        pairs = []
        for b in range(batches):
            for t in range(parts):
                there = to(b, t // 2, t % 2)
                pairs.append((b * parts + t, there[0] * parts + there[1] * 2 + there[2]))
        return lax.ppermute(a, ALL, pairs)

    over_core = lambda b, x, c: (b, x, 1 - c)
    over_x = lambda b, x, c: (b, 1 - x, c)
    u = lax.dynamic_index_in_dim(embeddings, core, 0, keepdims=False)
    out_shapes = [shape(half, width), shape(1, half)]
    codes = spread_code[None, :]

    if batches != 8 or parts != 4:
        whole = lax.all_gather(u, "batch", axis=0, tiled=True)
        theirs = send(level_index, over_x)
        stats, strip = call(
            functools.partial(first_kernel, False),
            [shape(8, total), shape(rows, total)],
            [pltpu.VMEM((1, total, TILE), jnp.float32)],
            56,
            codes,
            whole,
        )
        lane = jnp.arange(total)[None, :]
        line = jnp.where(lane < 128, level_index[0], theirs[0]).astype(jnp.float32)
        stats = jnp.concatenate([stats[: 1 + CODES], line])
        share = lambda c: lax.dynamic_slice_in_dim(strip, c * half, half)
        keep = jnp.concatenate([share(core), stats])
        recv = send(jnp.concatenate([share(1 - core), stats]), over_core)
        student = jnp.where(core == 1, whole, send(whole, over_core))
        out, loss = call(
            wide_mix_kernel,
            out_shapes,
            [pltpu.VMEM((3, block, 8), jnp.float32)],
            56,
            codes,
            keep,
            recv,
            student,
        )
        return out, loss[0]

    near = lambda b, x, c: (b ^ 2, x, c)
    far = lambda b, x, c: (b ^ 4, x, c)
    over_y = lambda b, x, c: (b ^ 1, x, c)
    turn = lambda b, x, c: (over_y if c else over_x)(b, x, c)
    return_turn = lambda b, x, c: (over_x if c else over_y)(b, x, c)
    level = jnp.broadcast_to(level_index.astype(jnp.bfloat16), (16, width))
    f = send(lax.dynamic_slice_in_dim(u, x * rows, rows, 0), far)
    n = send(u, near)
    y = send(u, over_y)
    g = send(f, near)
    ny = send(join([y], g), near)
    fa = send(join([f, level]), turn)
    fb = send(join([f, fa[:rows], level], g), return_turn)
    ga = send(g, turn)
    sooner = send(join([u, y, n, f, g], fa), over_core)
    some, head = 4 * block, 6 * block
    codes, a_stats, a_strip, a_rows = call(
        functools.partial(first_kernel, True),
        [
            shape(1, total, dtype=jnp.int32),
            shape(8, some),
            shape(rows, some),
            shape(some, width, dtype=jnp.bfloat16),
        ],
        [slots(some, some)],
        16,
        codes,
        u,
        y,
        n,
        f,
        g,
    )
    gb = send(join([g, ga], sooner, a_stats), return_turn)
    b_stats, b_strip, b_rows = call(
        second_kernel,
        [shape(8, head), shape(rows, head), shape(head, width, dtype=jnp.bfloat16)],
        [slots(head, head - some), slots(head - some, some)],
        16,
        codes,
        a_rows,
        a_stats,
        a_strip,
        fa,
        fb,
        ga,
    )
    c_stats, c_strip = call(
        third_kernel,
        [shape(8, total - block), shape(rows, total - block)],
        [slots(total - block, block), slots(block, head)],
        16,
        codes,
        b_rows,
        b_stats,
        b_strip,
        ny,
    )
    later = send(
        join([b_rows[some : some + 3 * rows], gb[:rows], ny, ga, gb[rows:]], c_stats), over_core
    )
    keep, mail = call(
        last_kernel,
        [shape(half + 8, total), shape(half + 8, total)],
        [pltpu.VMEM((block, total), jnp.float32), pltpu.VMEM((block, 8), jnp.float32)],
        16,
        codes,
        b_rows,
        ny,
        c_stats,
        c_strip,
        level_index,
        fa,
        fb,
        gb,
    )
    recv = send(mail, over_core)
    out, loss = call(
        mix_kernel,
        out_shapes,
        [pltpu.VMEM((3, block, 8), jnp.float32)],
        16,
        codes,
        keep,
        recv,
        b_rows,
        ny,
        gb,
        sooner,
        later,
    )
    return out, loss[0]


def solution(mesh):
    in_specs = (P(None, "batch", None), P(), P("temp"))
    out_specs = (P(("batch", "temp"), None), P(("batch", "temp")))
    return jax.shard_map(
        functools.partial(shards, mesh),
        mesh=mesh,
        in_specs=in_specs,
        out_specs=out_specs,
        check_vma=False,
    )
```

```python
import functools

import jax
import jax.numpy as jnp
from jax import lax
from jax.experimental import pallas as pl
from jax.experimental.pallas import tpu as pltpu
from jax.sharding import PartitionSpec as P

WEIGHT = 16.0
NEG = -1e30
LOG2E = 1.4426950408889634
CODES = 6
TILE = 256
CHUNK = 128
SPAN = 1024
ALL = ("batch", "temp")
SMEM = pl.BlockSpec(memory_space=pltpu.SMEM)
VMEM = pl.BlockSpec(memory_space=pltpu.VMEM)


def carried(count, body, carry):
    if count <= 8:
        for i in range(count):
            carry = body(i, carry)
        return carry
    return lax.fori_loop(0, count, body, carry)


def at(i, size):
    return pl.ds(i * size if isinstance(i, int) else pl.multiple_of(i * size, size), size)


def widths(code, width):
    root = jnp.sqrt(jnp.float32(width))
    return [jnp.exp2(0.5 * (code - jnp.float32(level))) / root for level in range(CODES)]


def powers(d, widest, wide):
    e = [None] * CODES
    e[5], e[4] = jnp.exp2(d * widest), jnp.exp2(d * wide)
    for level in (3, 2, 1, 0):
        e[level] = e[level + 2] * e[level + 2]
    return e


def columns(gram, count, bases):
    size = min(CHUNK, count)
    steps = count // size
    tile = gram.shape[1]
    best = carried(
        steps,
        lambda i, best: jnp.maximum(best, jnp.max(gram[at(i, size), :], axis=0, keepdims=True)),
        jnp.full((1, tile), NEG, jnp.float32),
    )

    def add(i, sums):
        e = powers(gram[at(i, size), :] - best, *bases)
        return tuple(s + jnp.sum(v, axis=0, keepdims=True) for s, v in zip(sums, e))

    return best, carried(steps, add, (jnp.zeros((1, tile), jnp.float32),) * CODES)


def times(a, b):
    return lax.dot_general(a, b, (((1,), (1,)), ((), ())), preferred_element_type=jnp.float32)


def hide_diagonal(gram, rows):
    square = gram[rows, :]
    own = lax.broadcasted_iota(jnp.int32, square.shape, 0) == lax.broadcasted_iota(
        jnp.int32, square.shape, 1
    )
    gram[rows, :] = jnp.where(own, NEG, square)


def bases_of(code, width):
    beta = widths(code.astype(jnp.float32), width)
    return beta[5] * LOG2E, beta[4] * LOG2E


def tiles(total):
    return [(i, min(TILE, total - i)) for i in range(0, total, TILE)]


def position():
    part = lax.axis_index("temp")
    return lax.axis_index("batch"), part // 2, part % 2


def spot(i, size):
    return pl.ds(pl.multiple_of(i * size, size), size)


def order_codes(spread, line, block):
    me, x, core = position()
    half = block // 2
    cut = [spread[:, spot(me ^ m, block)] for m in range(8)]
    cut[4:] = [jnp.where(x == 0, v, pltpu.roll(v, half, 1)) for v in cut[4:]]
    left = lax.broadcasted_iota(jnp.int32, cut[0].shape, 1) < half
    other = [None] * 4 + [pltpu.roll(v, half, 1) for v in cut[4:]]
    even = core == 0
    order = cut[:3] + [
        jnp.where(left, cut[4], other[6]),
        jnp.where(left, other[4], other[5]),
        jnp.where(left, other[5], jnp.where(even, cut[6], other[7])),
        cut[3],
        jnp.where(left, jnp.where(even, cut[7], other[6]), cut[7]),
    ]
    for m, v in enumerate(order):
        line[:, m * block : (m + 1) * block] = v


def first_kernel(staged, spread, *refs):
    me, x, core = position()
    if staged:
        *pieces, codes, stats, strip, whole, gram = refs
        block = pieces[0].shape[0]
        order_codes(spread, codes, block)
        row = 0
        for piece in pieces:
            whole[row : row + piece.shape[0], :] = piece[...]
            row += piece.shape[0]
        first_row = x * (block // 2)
    else:
        whole, stats, strip, gram = refs
        codes, block = spread, strip.shape[0] * 2
        first_row = me * block + x * (block // 2)
    total, width = whole.shape
    mine = pl.ds(pl.multiple_of(first_row, block // 2), block // 2)

    def tile(cols, size, slot=0):
        part = gram.at[slot, :, 0:size]
        part[...] = times(whole[...], whole[cols, :])
        hide_diagonal(part, cols)
        strip[:, cols] = part[mine, :]
        best, sums = columns(part, total, bases_of(codes[:, cols], width))
        stats[0:1, cols] = best
        for level in range(CODES):
            stats[1 + level : 2 + level, cols] = sums[level]
        stats[1 + CODES :, cols] = jnp.zeros((stats.shape[0] - 1 - CODES, size), jnp.float32)

    if staged:
        for slot, (start, size) in enumerate(tiles(total)):
            tile(pl.ds(start, size), size, slot)
    else:

        @pl.loop(0, total // TILE)
        def _(i):
            tile(at(i, TILE), TILE)


def swapped(a, block):
    left, right = a[:, -3 * block : -2 * block], a[:, -block:]
    half = block // 2
    low = lax.broadcasted_iota(jnp.int32, left.shape, 1) < half
    return jnp.where(low, left, pltpu.roll(right, half, 1)), jnp.where(
        low, pltpu.roll(left, half, 1), right
    )


def add_rows(codes, early, late, before, stats, strip, wide, square):
    tail, width = late.shape
    head, block = before.shape[1], 2 * strip.shape[0]
    last = slice(head, head + tail)
    row = 0
    for part in early:
        wide[:, row : row + part.shape[0]] = times(late[...], part[...])
        row += part.shape[0]
    gram = times(late[...], late[...])
    lines, lanes = (lax.broadcasted_iota(jnp.int32, gram.shape, axis) for axis in (0, 1))
    wide[:, last] = jnp.where(lines == lanes, NEG, gram)
    square[...] = jnp.broadcast_to(codes[:, last], (8, tail)).astype(jnp.float32).T
    bases = bases_of(square[:, 0:1], width)
    best = jnp.max(wide[...], axis=1, keepdims=True)
    part = powers(wide[...] - best, *bases)
    square[:, 0:1] = best
    for level in range(CODES):
        square[:, 1 + level : 2 + level] = jnp.sum(part[level], axis=1, keepdims=True)
    stats[:, last] = square[...].T
    for start, size in tiles(head):
        cols = pl.ds(start, size)
        bases = bases_of(codes[:, cols], width)
        best, sums = columns(wide.at[:, cols], tail, bases)
        top = jnp.maximum(best, before[0:1, cols])
        was, now = powers(before[0:1, cols] - top, *bases), powers(best - top, *bases)
        stats[0:1, cols] = top
        for level in range(CODES):
            stats[1 + level : 2 + level, cols] = (
                before[1 + level : 2 + level, cols] * was[level] + sums[level] * now[level]
            )
    _, x, _ = position()
    turned = wide[:, 0:block].T
    strip[:, last] = jnp.where(x == 0, turned[: block // 2], turned[block // 2 :])


def second_kernel(codes, early, before, part_strip, fa, fb, ga, stats, strip, whole, wide, square):
    _, x, core = position()
    head, half = early.shape[0], ga.shape[0]
    late = whole.at[head:, :]
    late[spot(core, half), :] = fa[0:half, :]
    late[spot(1 - core, half), :] = fb[0:half, :]
    late[2 * half : 3 * half, :] = fb[half : 2 * half, :]
    late[3 * half : 4 * half, :] = ga[...]
    whole[0:head, :] = early[...]
    strip[:, 0:head] = part_strip[...]
    add_rows(codes, [early], late, before, stats, strip, wide, square)
    stats[1 + CODES :, :] = jnp.zeros((stats.shape[0] - 1 - CODES, stats.shape[1]), jnp.float32)


def third_kernel(codes, early, before, part_strip, late, stats, strip, wide, square):
    strip[:, 0 : early.shape[0]] = part_strip[...]
    add_rows(codes, [early], late, before, stats, strip, wide, square)
    stats[1 + CODES :, :] = jnp.zeros((stats.shape[0] - 1 - CODES, stats.shape[1]), jnp.float32)


def last_kernel(
    codes, early, middle, before, part_strip, level_index, fa, fb, late, keep, send, strip, wide, square
):
    _, x, core = position()
    block = late.shape[0]
    half = block // 4
    strip[:, 0 : before.shape[1]] = part_strip[...]
    stats = keep.at[half:, :]
    add_rows(codes, [early, middle], late, before, stats, strip, wide, square)
    lane = lax.broadcasted_iota(jnp.int32, (1, stats.shape[1]), 1)
    level = level_index[0].astype(jnp.float32)
    theirs = jnp.where(core == 0, fa[block // 2 : block // 2 + 1, 0:1], fb[block : block + 1, 0:1])
    stats[1 + CODES :, :] = jnp.where(lane < 128, level, theirs.astype(jnp.float32))
    keep[0:half, :] = strip[spot(core, half), :]
    send[0:half, :] = strip[spot(1 - core, half), :]
    send[half:, :] = stats[...]
    left, right = swapped(send, block)
    send[:, -3 * block : -2 * block] = left
    send[:, -block:] = right


class Mixer:
    def __init__(self, own, width, codes, keep, recv, turned):
        _, x, core = position()
        self.codes, self.width = codes, width
        self.rows = rows = keep.shape[0] - 8
        self.student = core == 1
        self.keep, self.recv = keep, recv
        block = 4 * rows
        own = spot(own, block)
        code = codes[:, own].astype(jnp.float32)
        turned[0] = self.pick(rows, rows + 8, own, True).T
        turned[1] = self.pick(rows, rows + 8, own, False).T
        turned[2] = jnp.broadcast_to(code, (8, block)).T
        mine = spot(2 * x + core, rows)
        s, t = turned[0, mine, :], turned[1, mine, :]
        self.beta = widths(turned[2, mine, 0:1], width)
        found = [
            ref[rows + 1 + CODES : rows + 2 + CODES, lane : lane + 1]
            for ref in (keep, recv)
            for lane in (0, 128)
        ]
        self.count = [sum(jnp.where(v == jnp.float32(c), 1.0, 0.0) for v in found) for c in range(CODES)]
        self.s_top, self.t_top = s[:, 0:1], t[:, 0:1]
        self.s_sum = [s[:, 1 + c : 2 + c] for c in range(CODES)]
        self.t_sum = [t[:, 1 + c : 2 + c] for c in range(CODES)]

    def pick(self, low, high, cols, student):
        here, there = self.keep[low:high, cols], self.recv[low:high, cols]
        return jnp.where(self.student == student, here, there)

    def weighted(self, d, beta, sums):
        e = powers(d, beta[5] * LOG2E, beta[4] * LOG2E)
        return sum(v * (n * b / s) for v, n, b, s in zip(e, self.count, beta, sums))

    def part(self, cols):
        rows = self.rows
        gs, gt = self.pick(0, rows, cols, True), self.pick(0, rows, cols, False)
        s, t = self.pick(rows, rows + 8, cols, True), self.pick(rows, rows + 8, cols, False)
        beta = widths(self.codes[:, cols].astype(jnp.float32), self.width)
        lines = lambda a: [a[1 + c : 2 + c] for c in range(CODES)]
        p_row = self.weighted(gt - self.t_top, self.beta, self.t_sum)
        q_row = self.weighted(gs - self.s_top, self.beta, self.s_sum)
        p_col = self.weighted(gt - t[0:1], beta, lines(t))
        q_col = self.weighted(gs - s[0:1], beta, lines(s))
        mix = WEIGHT * ((q_row - p_row) + (q_col - p_col))
        return mix.astype(jnp.bfloat16), jnp.sum(p_row * (gt - gs), axis=1, keepdims=True)

    def store_loss(self, loss, out):
        for c in range(CODES):
            loss = loss + self.count[c] * (
                self.beta[c] * (self.s_top - self.t_top)
                + (jnp.log(self.s_sum[c]) - jnp.log(self.t_sum[c]))
            )
        out[...] = jnp.broadcast_to(loss, (self.rows, 128)).T[0:1, :]


def product(a, b):
    return jnp.dot(a, b, preferred_element_type=jnp.float32)


def mix_kernel(codes, keep, recv, early, middle, late, sooner, later, out, loss, turned):
    mixer = Mixer(0, out.shape[1], codes, keep, recv, turned)
    mix, gap = mixer.part(pl.ds(0, codes.shape[1]))
    mixer.store_loss(gap, loss)

    def against(*parts):
        row, total = 0, None
        for part in parts:
            term = product(mix[:, row : row + part.shape[0]], part[...])
            row, total = row + part.shape[0], term if total is None else total + term
        out[...] = total

    @pl.when(mixer.student)
    def _():
        against(early, middle, late)

    @pl.when(jnp.logical_not(mixer.student))
    def _():
        against(sooner, later)


def wide_mix_kernel(codes, keep, recv, student, out, loss, turned):
    total, width = student.shape
    mixer = Mixer(lax.axis_index("batch"), width, codes, keep, recv, turned)
    span = min(SPAN, total)

    def step(i, carry):
        mix, gap = mixer.part(at(i, span))
        return carry[0] + product(mix, student[at(i, span), :]), carry[1] + gap

    zero = jnp.zeros((mixer.rows, width), jnp.float32), jnp.zeros((mixer.rows, 1), jnp.float32)
    out[...], gap = lax.fori_loop(0, total // span, step, zero)
    mixer.store_loss(gap, loss)


def call(kernel, shapes, scratch, limit, *args):
    return pl.pallas_call(
        kernel,
        out_shape=shapes,
        in_specs=[SMEM if a.shape == (1,) else VMEM for a in args],
        out_specs=[VMEM] * len(shapes),
        scratch_shapes=scratch,
        compiler_params=pltpu.CompilerParams(vmem_limit_bytes=limit << 20),
    )(*args)


def room(rows, cols):
    return [pltpu.VMEM((rows, cols), jnp.float32), pltpu.VMEM((rows, 8), jnp.float32)]


def join(parts, *behind):
    def kernel(*refs):
        row = 0
        for part in refs[: len(parts)]:
            refs[-1][row : row + part.shape[0], :] = part[...]
            row += part.shape[0]

    dims = sum(p.shape[0] for p in parts), parts[0].shape[1]
    return call(kernel, [shape(*dims, dtype=parts[0].dtype)], [], 16, *parts, *behind)[0]


def shape(*dims, dtype=jnp.float32):
    return jax.ShapeDtypeStruct(dims, dtype)


def shards(mesh, embeddings, spread_code, level_index):
    block, width = embeddings.shape[1:]
    batches, parts = mesh.shape["batch"], mesh.shape["temp"]
    total = block * batches
    me, part = lax.axis_index("batch"), lax.axis_index("temp")
    x, core = part // 2, part % 2
    rows, half = block // 2, block // 4

    def send(a, to):
        pairs = []
        for b in range(batches):
            for t in range(parts):
                there = to(b, t // 2, t % 2)
                pairs.append((b * parts + t, there[0] * parts + there[1] * 2 + there[2]))
        return lax.ppermute(a, ALL, pairs)

    over_core = lambda b, x, c: (b, x, 1 - c)
    over_x = lambda b, x, c: (b, 1 - x, c)
    u = lax.dynamic_index_in_dim(embeddings, core, 0, keepdims=False)
    out_shapes = [shape(half, width), shape(1, half)]
    codes = spread_code[None, :]

    if batches != 8 or parts != 4:
        whole = lax.all_gather(u, "batch", axis=0, tiled=True)
        theirs = send(level_index, over_x)
        stats, strip = call(
            functools.partial(first_kernel, False),
            [shape(8, total), shape(rows, total)],
            [pltpu.VMEM((1, total, TILE), jnp.float32)],
            56,
            codes,
            whole,
        )
        lane = jnp.arange(total)[None, :]
        line = jnp.where(lane < 128, level_index[0], theirs[0]).astype(jnp.float32)
        stats = jnp.concatenate([stats[: 1 + CODES], line])
        share = lambda c: lax.dynamic_slice_in_dim(strip, c * half, half)
        keep = jnp.concatenate([share(core), stats])
        recv = send(jnp.concatenate([share(1 - core), stats]), over_core)
        student = jnp.where(core == 1, whole, send(whole, over_core))
        out, loss = call(
            wide_mix_kernel,
            out_shapes,
            [pltpu.VMEM((3, block, 8), jnp.float32)],
            56,
            codes,
            keep,
            recv,
            student,
        )
        return out, loss[0]

    near = lambda b, x, c: (b ^ 2, x, c)
    far = lambda b, x, c: (b ^ 4, x, c)
    over_y = lambda b, x, c: (b ^ 1, x, c)
    turn = lambda b, x, c: (over_y if c else over_x)(b, x, c)
    return_turn = lambda b, x, c: (over_x if c else over_y)(b, x, c)
    level = jnp.broadcast_to(level_index.astype(jnp.bfloat16), (16, width))
    f = send(lax.dynamic_slice_in_dim(u, x * rows, rows, 0), far)
    n = send(u, near)
    y = send(u, over_y)
    g = send(f, near)
    ny = send(join([y], g), near)
    fa = send(join([f, level]), turn)
    fb = send(join([f, fa[:rows], level], g), return_turn)
    ga = send(g, turn)
    sooner = send(join([u, y, n, f, g], fa), over_core)
    some, head = 4 * block, 6 * block
    codes, a_stats, a_strip, a_rows = call(
        functools.partial(first_kernel, True),
        [
            shape(1, total, dtype=jnp.int32),
            shape(8, some),
            shape(rows, some),
            shape(some, width, dtype=jnp.bfloat16),
        ],
        [pltpu.VMEM((some // TILE, some, TILE), jnp.float32)],
        16,
        codes,
        u,
        y,
        n,
        f,
        g,
    )
    gb = send(join([g, ga], sooner, a_stats), return_turn)
    b_stats, b_strip, b_rows = call(
        second_kernel,
        [shape(8, head), shape(rows, head), shape(head, width, dtype=jnp.bfloat16)],
        room(head - some, head),
        16,
        codes,
        a_rows,
        a_stats,
        a_strip,
        fa,
        fb,
        ga,
    )
    c_stats, c_strip = call(
        third_kernel,
        [shape(8, total - block), shape(rows, total - block)],
        room(block, total - block),
        16,
        codes,
        b_rows,
        b_stats,
        b_strip,
        ny,
    )
    later = send(
        join([b_rows[some : some + 3 * rows], gb[:rows], ny, ga, gb[rows:]], c_stats), over_core
    )
    keep, mail = call(
        last_kernel,
        [shape(half + 8, total), shape(half + 8, total)],
        [pltpu.VMEM((rows, total), jnp.float32)] + room(block, total),
        16,
        codes,
        b_rows,
        ny,
        c_stats,
        c_strip,
        level_index,
        fa,
        fb,
        gb,
    )
    recv = send(mail, over_core)
    out, loss = call(
        mix_kernel,
        out_shapes,
        [pltpu.VMEM((3, block, 8), jnp.float32)],
        16,
        codes,
        keep,
        recv,
        b_rows,
        ny,
        gb,
        sooner,
        later,
    )
    return out, loss[0]


def solution(mesh):
    in_specs = (P(None, "batch", None), P(), P("temp"))
    out_specs = (P(("batch", "temp"), None), P(("batch", "temp")))
    return jax.shard_map(
        functools.partial(shards, mesh),
        mesh=mesh,
        in_specs=in_specs,
        out_specs=out_specs,
        check_vma=False,
    )
```

```python
import functools

import jax
import jax.numpy as jnp
from jax import lax
from jax.experimental import pallas as pl
from jax.experimental.pallas import tpu as pltpu
from jax.sharding import PartitionSpec as P

WEIGHT = 16.0
NEG = -1e30
LOG2E = 1.4426950408889634
CODES = 6
TILE = 256
CHUNK = 128
SPAN = 1024
ALL = ("batch", "temp")
SMEM = pl.BlockSpec(memory_space=pltpu.SMEM)
VMEM = pl.BlockSpec(memory_space=pltpu.VMEM)


def carried(count, body, carry):
    if count <= 8:
        for i in range(count):
            carry = body(i, carry)
        return carry
    return lax.fori_loop(0, count, body, carry)


def at(i, size):
    return pl.ds(i * size if isinstance(i, int) else pl.multiple_of(i * size, size), size)


def widths(code, width):
    root = jnp.sqrt(jnp.float32(width))
    return [jnp.exp2(0.5 * (code - jnp.float32(level))) / root for level in range(CODES)]


def powers(d, widest, wide):
    e = [None] * CODES
    e[5], e[4] = jnp.exp2(d * widest), jnp.exp2(d * wide)
    for level in (3, 2, 1, 0):
        e[level] = e[level + 2] * e[level + 2]
    return e


def columns(gram, count, bases):
    size = min(CHUNK, count)
    steps = count // size
    tile = gram.shape[1]
    best = carried(
        steps,
        lambda i, best: jnp.maximum(best, jnp.max(gram[at(i, size), :], axis=0, keepdims=True)),
        jnp.full((1, tile), NEG, jnp.float32),
    )

    def add(i, sums):
        e = powers(gram[at(i, size), :] - best, *bases)
        return tuple(s + jnp.sum(v, axis=0, keepdims=True) for s, v in zip(sums, e))

    return best, carried(steps, add, (jnp.zeros((1, tile), jnp.float32),) * CODES)


def times(a, b):
    return lax.dot_general(a, b, (((1,), (1,)), ((), ())), preferred_element_type=jnp.float32)


def hide_diagonal(gram, rows):
    square = gram[rows, :]
    own = lax.broadcasted_iota(jnp.int32, square.shape, 0) == lax.broadcasted_iota(
        jnp.int32, square.shape, 1
    )
    gram[rows, :] = jnp.where(own, NEG, square)


def bases_of(code, width):
    beta = widths(code.astype(jnp.float32), width)
    return beta[5] * LOG2E, beta[4] * LOG2E


def tiles(total):
    return [(i, min(TILE, total - i)) for i in range(0, total, TILE)]


def position():
    part = lax.axis_index("temp")
    return lax.axis_index("batch"), part // 2, part % 2


def spot(i, size):
    return pl.ds(pl.multiple_of(i * size, size), size)


def order_codes(spread, line, block):
    me, x, core = position()
    half = block // 2
    cut = [spread[:, spot(me ^ m, block)] for m in range(8)]
    cut[4:] = [jnp.where(x == 0, v, pltpu.roll(v, half, 1)) for v in cut[4:]]
    left = lax.broadcasted_iota(jnp.int32, cut[0].shape, 1) < half
    other = [None] * 4 + [pltpu.roll(v, half, 1) for v in cut[4:]]
    even = core == 0
    order = [
        cut[0],
        cut[2],
        cut[1],
        jnp.where(left, cut[4], other[6]),
        jnp.where(left, other[4], other[5]),
        jnp.where(left, other[5], jnp.where(even, cut[6], other[7])),
        cut[3],
        jnp.where(left, jnp.where(even, cut[7], other[6]), cut[7]),
    ]
    for m, v in enumerate(order):
        line[:, m * block : (m + 1) * block] = v


def first_kernel(staged, spread, *refs):
    me, x, core = position()
    if staged:
        *pieces, codes, stats, strip, whole, gram = refs
        block = pieces[0].shape[0]
        order_codes(spread, codes, block)
        row = 0
        for piece in pieces:
            whole[row : row + piece.shape[0], :] = piece[...]
            row += piece.shape[0]
        first_row = x * (block // 2)
    else:
        whole, stats, strip, gram = refs
        codes, block = spread, strip.shape[0] * 2
        first_row = me * block + x * (block // 2)
    total, width = whole.shape
    mine = pl.ds(pl.multiple_of(first_row, block // 2), block // 2)

    def tile(cols, size, slot=0):
        part = gram.at[slot, :, 0:size]
        part[...] = times(whole[...], whole[cols, :])
        hide_diagonal(part, cols)
        strip[:, cols] = part[mine, :]
        best, sums = columns(part, total, bases_of(codes[:, cols], width))
        stats[0:1, cols] = best
        for level in range(CODES):
            stats[1 + level : 2 + level, cols] = sums[level]
        stats[1 + CODES :, cols] = jnp.zeros((stats.shape[0] - 1 - CODES, size), jnp.float32)

    if staged:
        for slot, (start, size) in enumerate(tiles(total)):
            tile(pl.ds(start, size), size, slot)
    else:

        @pl.loop(0, total // TILE)
        def _(i):
            tile(at(i, TILE), TILE)


def swapped(a, block):
    left, right = a[:, -3 * block : -2 * block], a[:, -block:]
    half = block // 2
    low = lax.broadcasted_iota(jnp.int32, left.shape, 1) < half
    return jnp.where(low, left, pltpu.roll(right, half, 1)), jnp.where(
        low, pltpu.roll(left, half, 1), right
    )


def add_rows(codes, early, late, before, stats, strip, wide, square):
    tail, width = late.shape
    head, block = before.shape[1], 2 * strip.shape[0]
    last = slice(head, head + tail)
    row = 0
    for part in early:
        wide[:, row : row + part.shape[0]] = times(late[...], part[...])
        row += part.shape[0]
    gram = times(late[...], late[...])
    lines, lanes = (lax.broadcasted_iota(jnp.int32, gram.shape, axis) for axis in (0, 1))
    wide[:, last] = jnp.where(lines == lanes, NEG, gram)
    square[...] = jnp.broadcast_to(codes[:, last], (8, tail)).astype(jnp.float32).T
    bases = bases_of(square[:, 0:1], width)
    best = jnp.max(wide[...], axis=1, keepdims=True)
    part = powers(wide[...] - best, *bases)
    square[:, 0:1] = best
    for level in range(CODES):
        square[:, 1 + level : 2 + level] = jnp.sum(part[level], axis=1, keepdims=True)
    stats[:, last] = square[...].T
    for start, size in tiles(head):
        cols = pl.ds(start, size)
        bases = bases_of(codes[:, cols], width)
        best, sums = columns(wide.at[:, cols], tail, bases)
        top = jnp.maximum(best, before[0:1, cols])
        was, now = powers(before[0:1, cols] - top, *bases), powers(best - top, *bases)
        stats[0:1, cols] = top
        for level in range(CODES):
            stats[1 + level : 2 + level, cols] = (
                before[1 + level : 2 + level, cols] * was[level] + sums[level] * now[level]
            )
    _, x, _ = position()
    turned = wide[:, 0:block].T
    strip[:, last] = jnp.where(x == 0, turned[: block // 2], turned[block // 2 :])


def second_kernel(
    codes, early, before, part_strip, level_index, fa, fb, ga, stats, strip, whole, level, wide, square
):
    _, x, core = position()
    head, half = early.shape[0], ga.shape[0]
    late = whole.at[head:, :]
    late[spot(core, half), :] = fa[0:half, :]
    late[spot(1 - core, half), :] = fb[0:half, :]
    late[2 * half : 3 * half, :] = fb[half : 2 * half, :]
    late[3 * half : 4 * half, :] = ga[...]
    whole[0:head, :] = early[...]
    strip[:, 0:head] = part_strip[...]
    add_rows(codes, [early], late, before, stats, strip, wide, square)
    stats[1 + CODES :, :] = jnp.zeros((stats.shape[0] - 1 - CODES, stats.shape[1]), jnp.float32)
    theirs = jnp.where(
        core == 0, fa[half : half + 1, 0:1], fb[2 * half : 2 * half + 1, 0:1]
    ).astype(jnp.float32)
    row = lax.broadcasted_iota(jnp.int32, level.shape, 0)
    level[...] = jnp.where(row == 0, level_index[0].astype(jnp.float32), theirs)


def third_kernel(codes, early, before, part_strip, late, _, stats, strip, wide, square):
    strip[:, 0 : early.shape[0]] = part_strip[...]
    add_rows(codes, [early], late, before, stats, strip, wide, square)
    stats[1 + CODES :, :] = jnp.zeros((stats.shape[0] - 1 - CODES, stats.shape[1]), jnp.float32)


def last_kernel(codes, early, middle, before, part_strip, late, keep, send, strip, wide, square):
    _, x, core = position()
    block = late.shape[0]
    half = block // 4
    strip[:, 0 : before.shape[1]] = part_strip[...]
    stats = keep.at[half:, :]
    add_rows(codes, [early, middle], late, before, stats, strip, wide, square)
    stats[1 + CODES :, :] = jnp.zeros((stats.shape[0] - 1 - CODES, stats.shape[1]), jnp.float32)
    keep[0:half, :] = strip[spot(core, half), :]
    send[0:half, :] = strip[spot(1 - core, half), :]
    send[half:, :] = stats[...]
    left, right = swapped(send, block)
    send[:, -3 * block : -2 * block] = left
    send[:, -block:] = right


def counted(*levels):
    row = lax.broadcasted_iota(jnp.int32, (8, 1), 0).astype(jnp.float32) - 1.0
    found = [ref[i : i + 1, 0:1] for ref in levels for i in (0, 1)]
    return sum(jnp.where(row == level, 1.0, 0.0) for level in found)


class Half:
    def __init__(self, own, width, codes, box, count, turned):
        _, x, core = position()
        rows = box.shape[0] - 8
        self.codes, self.width, self.count = codes, width, count
        self.gram, self.stats = box.at[0:rows, :], box.at[rows : rows + 8, :]
        own = spot(own, 4 * rows)
        beta, weight, stats = self.lines(own)
        row = lax.broadcasted_iota(jnp.int32, stats.shape, 0)
        inner = (row > 0) & (row <= CODES)
        lse = jnp.where(inner, count * (beta * stats[0:1] + jnp.log(stats)), 0.0)
        lse = jnp.sum(lse, axis=0, keepdims=True)
        turned[0] = jnp.where(inner, weight, jnp.where(row == 0, stats, lse)).T
        turned[1] = (beta * LOG2E).T
        mine = spot(2 * x + core, rows)
        lead, base = turned[0, mine, :], turned[1, mine, :]
        self.top, self.lse = lead[:, 0:1], lead[:, 7:8]
        self.weight = [lead[:, 1 + c : 2 + c] for c in range(CODES)]
        self.bases = base[:, 6:7], base[:, 5:6]

    def lines(self, cols):
        stats = self.stats[:, cols]
        row = lax.broadcasted_iota(jnp.int32, stats.shape, 0)
        code = self.codes[:, cols].astype(jnp.float32)
        beta = jnp.exp2(0.5 * (code - (row.astype(jnp.float32) - 1.0))) / jnp.sqrt(
            jnp.float32(self.width)
        )
        stats = jnp.where((row > CODES), 1.0, stats)
        return beta, self.count * beta / jnp.where(row == 0, 1.0, stats), stats

    def part(self, cols):
        gram = self.gram[:, cols]
        beta, weight, stats = self.lines(cols)
        by_row = sum(v * w for v, w in zip(powers(gram - self.top, *self.bases), self.weight))
        e = powers(gram - stats[0:1], beta[6:7] * LOG2E, beta[5:6] * LOG2E)
        by_col = sum(v * weight[1 + c : 2 + c] for c, v in enumerate(e))
        return by_row, by_row + by_col


def product(a, b):
    return jnp.dot(a, b, preferred_element_type=jnp.float32)


def store_loss(gap, difference, out):
    out[...] = jnp.broadcast_to(gap + difference, (gap.shape[0], 128)).T[0:1, :]


def half_kernel(width, codes, keep, level, their_level, by_row, both, lse, turned):
    half = Half(0, width, codes, keep, counted(level, their_level), turned)
    by_row[...], both[...] = half.part(pl.ds(0, codes.shape[1]))
    lse[...] = jnp.broadcast_to(half.lse, lse.shape)


def mix_kernel(
    codes, keep, recv, level, their_level, by_row, both, lse, early, middle, late, sooner, later,
    out, loss, turned
):
    half = Half(0, out.shape[1], codes, recv, counted(level, their_level), turned)
    student = position()[2] == 1
    their_row, their_both = half.part(pl.ds(0, codes.shape[1]))
    sign = jnp.where(student, 1.0, -1.0)
    mix = ((WEIGHT * sign) * (both[...] - their_both)).astype(jnp.bfloat16)
    rows = by_row.shape[0]
    p_row = jnp.where(student, their_row, by_row[...])
    gap = jnp.sum(p_row * (recv[0:rows, :] - keep[0:rows, :]), axis=1, keepdims=True)
    store_loss(sign * gap, sign * (lse[:, 0:1] - half.lse), loss)

    def against(*parts):
        row, total = 0, None
        for part in parts:
            term = product(mix[:, row : row + part.shape[0]], part[...])
            row, total = row + part.shape[0], term if total is None else total + term
        out[...] = total

    @pl.when(student)
    def _():
        against(early, middle, late)

    @pl.when(jnp.logical_not(student))
    def _():
        against(sooner, later)


def wide_mix_kernel(codes, s_box, t_box, level, their_level, student, out, loss, turned):
    total, width = student.shape
    own, count = lax.axis_index("batch"), counted(level, their_level)
    s = Half(own, width, codes, s_box, count, turned.at[0:2])
    t = Half(own, width, codes, t_box, count, turned.at[2:4])
    span, rows = min(SPAN, total), out.shape[0]

    def step(i, carry):
        cols = at(i, span)
        (_, q), (p_row, p) = s.part(cols), t.part(cols)
        gap = jnp.sum(p_row * (t_box[0:rows, cols] - s_box[0:rows, cols]), axis=1, keepdims=True)
        mix = (WEIGHT * (q - p)).astype(jnp.bfloat16)
        return carry[0] + product(mix, student[cols, :]), carry[1] + gap

    zero = jnp.zeros((rows, width), jnp.float32), jnp.zeros((rows, 1), jnp.float32)
    out[...], gap = lax.fori_loop(0, total // span, step, zero)
    store_loss(gap, s.lse - t.lse, loss)


def call(kernel, shapes, scratch, limit, *args):
    return pl.pallas_call(
        kernel,
        out_shape=shapes,
        in_specs=[SMEM if a.shape == (1,) else VMEM for a in args],
        out_specs=[VMEM] * len(shapes),
        scratch_shapes=scratch,
        compiler_params=pltpu.CompilerParams(vmem_limit_bytes=limit << 20),
    )(*args)


def room(rows, cols):
    return [pltpu.VMEM((rows, cols), jnp.float32), pltpu.VMEM((rows, 8), jnp.float32)]


def join(parts, *behind):
    def kernel(*refs):
        row = 0
        for part in refs[: len(parts)]:
            refs[-1][row : row + part.shape[0], :] = part[...]
            row += part.shape[0]

    dims = sum(p.shape[0] for p in parts), parts[0].shape[1]
    return call(kernel, [shape(*dims, dtype=parts[0].dtype)], [], 16, *parts, *behind)[0]


def shape(*dims, dtype=jnp.float32):
    return jax.ShapeDtypeStruct(dims, dtype)


def shards(mesh, embeddings, spread_code, level_index):
    block, width = embeddings.shape[1:]
    batches, parts = mesh.shape["batch"], mesh.shape["temp"]
    total = block * batches
    me, part = lax.axis_index("batch"), lax.axis_index("temp")
    x, core = part // 2, part % 2
    rows, half = block // 2, block // 4

    def send(a, to):
        pairs = []
        for b in range(batches):
            for t in range(parts):
                there = to(b, t // 2, t % 2)
                pairs.append((b * parts + t, there[0] * parts + there[1] * 2 + there[2]))
        return lax.ppermute(a, ALL, pairs)

    over_core = lambda b, x, c: (b, x, 1 - c)
    over_x = lambda b, x, c: (b, 1 - x, c)
    u = lax.dynamic_index_in_dim(embeddings, core, 0, keepdims=False)
    out_shapes = [shape(half, width), shape(1, half)]
    codes = spread_code[None, :]

    if batches != 8 or parts != 4:
        whole = lax.all_gather(u, "batch", axis=0, tiled=True)
        theirs = send(level_index, over_x)
        stats, strip = call(
            functools.partial(first_kernel, False),
            [shape(8, total), shape(rows, total)],
            [pltpu.VMEM((1, total, TILE), jnp.float32)],
            56,
            codes,
            whole,
        )
        level = jnp.stack([level_index, theirs] + [theirs] * 6).astype(jnp.float32)
        level = jnp.broadcast_to(level, (8, 128))
        share = lambda c: lax.dynamic_slice_in_dim(strip, c * half, half)
        keep = jnp.concatenate([share(core), stats])
        recv = send(jnp.concatenate([share(1 - core), stats]), over_core)
        student = jnp.where(core == 1, whole, send(whole, over_core))
        out, loss = call(
            wide_mix_kernel,
            out_shapes,
            [pltpu.VMEM((4, block, 8), jnp.float32)],
            56,
            codes,
            jnp.where(core == 1, keep, recv),
            jnp.where(core == 1, recv, keep),
            level,
            send(level, over_core),
            student,
        )
        return out, loss[0]

    near = lambda b, x, c: (b ^ 2, x, c)
    far = lambda b, x, c: (b ^ 4, x, c)
    over_y = lambda b, x, c: (b ^ 1, x, c)
    turn = lambda b, x, c: (over_y if c else over_x)(b, x, c)
    return_turn = lambda b, x, c: (over_x if c else over_y)(b, x, c)
    level = jnp.broadcast_to(level_index.astype(jnp.bfloat16), (16, width))
    f = send(lax.dynamic_slice_in_dim(u, x * rows, rows, 0), far)
    n = send(u, near)
    y = send(u, over_y)
    g = send(f, near)
    ny = send(join([y], g), near)
    fa = send(join([f, level]), turn)
    fb = send(join([f, fa[:rows], level], g), return_turn)
    ga = send(g, turn)
    sooner = send(join([join([u, n]), y, f, g], fa), over_core)
    some, head = 4 * block, 6 * block
    codes, a_stats, a_strip, a_rows = call(
        functools.partial(first_kernel, True),
        [
            shape(1, total, dtype=jnp.int32),
            shape(8, some),
            shape(rows, some),
            shape(some, width, dtype=jnp.bfloat16),
        ],
        [pltpu.VMEM((some // TILE, some, TILE), jnp.float32)],
        16,
        codes,
        u,
        n,
        y,
        f,
        g,
    )
    gb = send(join([g, ga], sooner, a_stats), return_turn)
    b_stats, b_strip, b_rows, levels = call(
        second_kernel,
        [
            shape(8, head),
            shape(rows, head),
            shape(head, width, dtype=jnp.bfloat16),
            shape(8, 128),
        ],
        room(head - some, head),
        16,
        codes,
        a_rows,
        a_stats,
        a_strip,
        level_index,
        fa,
        fb,
        ga,
    )
    their_levels = send(levels, over_core)
    c_stats, c_strip = call(
        third_kernel,
        [shape(8, total - block), shape(rows, total - block)],
        room(block, total - block),
        16,
        codes,
        b_rows,
        b_stats,
        b_strip,
        ny,
        their_levels,
    )
    later = send(
        join([b_rows[some : some + 3 * rows], gb[:rows], ny, ga, gb[rows:]], c_stats), over_core
    )
    keep, mail = call(
        last_kernel,
        [shape(half + 8, total), shape(half + 8, total)],
        [pltpu.VMEM((rows, total), jnp.float32)] + room(block, total),
        16,
        codes,
        b_rows,
        ny,
        c_stats,
        c_strip,
        gb,
    )
    recv = send(mail, over_core)
    by_row, both, lse = call(
        functools.partial(half_kernel, width),
        [shape(half, total), shape(half, total), shape(half, 8)],
        [pltpu.VMEM((2, block, 8), jnp.float32)],
        16,
        codes,
        keep,
        levels,
        their_levels,
    )
    out, loss = call(
        mix_kernel,
        out_shapes,
        [pltpu.VMEM((2, block, 8), jnp.float32)],
        16,
        codes,
        keep,
        recv,
        levels,
        their_levels,
        by_row,
        both,
        lse,
        b_rows,
        ny,
        gb,
        sooner,
        later,
    )
    return out, loss[0]


def solution(mesh):
    in_specs = (P(None, "batch", None), P(), P("temp"))
    out_specs = (P(("batch", "temp"), None), P(("batch", "temp")))
    return jax.shard_map(
        functools.partial(shards, mesh),
        mesh=mesh,
        in_specs=in_specs,
        out_specs=out_specs,
        check_vma=False,
    )
```

```python
import functools

import jax
import jax.numpy as jnp
from jax import lax
from jax.experimental import pallas as pl
from jax.experimental.pallas import tpu as pltpu
from jax.sharding import PartitionSpec as P

WEIGHT = 16.0
NEG = -1e30
LOG2E = 1.4426950408889634
CODES = 6
TILE = 256
CHUNK = 128
SPAN = 1024
ALL = ("batch", "temp")
SMEM = pl.BlockSpec(memory_space=pltpu.SMEM)
VMEM = pl.BlockSpec(memory_space=pltpu.VMEM)


def carried(count, body, carry):
    if count <= 8:
        for i in range(count):
            carry = body(i, carry)
        return carry
    return lax.fori_loop(0, count, body, carry)


def at(i, size):
    return pl.ds(i * size if isinstance(i, int) else pl.multiple_of(i * size, size), size)


def widths(code, width):
    root = jnp.sqrt(jnp.float32(width))
    return [jnp.exp2(0.5 * (code - jnp.float32(level))) / root for level in range(CODES)]


def powers(d, widest, wide):
    e = [None] * CODES
    e[5], e[4] = jnp.exp2(d * widest), jnp.exp2(d * wide)
    for level in (3, 2, 1, 0):
        e[level] = e[level + 2] * e[level + 2]
    return e


def columns(gram, count, bases):
    size = min(CHUNK, count)
    tile = gram.shape[1]

    def lines(i):
        for j in range(0, size, 8):
            start = i * size + j
            yield gram[pl.ds(start if isinstance(i, int) else pl.multiple_of(start, 8), 8), :]

    def top(i, best):
        for line in lines(i):
            best = jnp.maximum(best, line)
        return best

    best = carried(count // size, top, jnp.full((8, tile), NEG, jnp.float32))
    best = jnp.max(best, axis=0, keepdims=True)

    def add(i, sums):
        for line in lines(i):
            sums = tuple(s + v for s, v in zip(sums, powers(line - best, *bases)))
        return sums

    sums = carried(count // size, add, (jnp.zeros((8, tile), jnp.float32),) * CODES)
    return best, [jnp.sum(s, axis=0, keepdims=True) for s in sums]


def times(a, b):
    return lax.dot_general(a, b, (((1,), (1,)), ((), ())), preferred_element_type=jnp.float32)


def hide_diagonal(gram, rows):
    square = gram[rows, :]
    own = lax.broadcasted_iota(jnp.int32, square.shape, 0) == lax.broadcasted_iota(
        jnp.int32, square.shape, 1
    )
    gram[rows, :] = jnp.where(own, NEG, square)


def bases_of(code, width):
    beta = widths(code.astype(jnp.float32), width)
    return beta[5] * LOG2E, beta[4] * LOG2E


def tiles(total):
    return [(i, min(TILE, total - i)) for i in range(0, total, TILE)]


def position():
    part = lax.axis_index("temp")
    return lax.axis_index("batch"), part // 2, part % 2


def spot(i, size):
    return pl.ds(pl.multiple_of(i * size, size), size)


def order_codes(spread, line, block):
    me, x, core = position()
    half = block // 2
    cut = [spread[:, spot(me ^ m, block)] for m in range(8)]
    cut[4:] = [jnp.where(x == 0, v, pltpu.roll(v, half, 1)) for v in cut[4:]]
    left = lax.broadcasted_iota(jnp.int32, cut[0].shape, 1) < half
    other = [None] * 4 + [pltpu.roll(v, half, 1) for v in cut[4:]]
    even = core == 0
    order = [
        cut[0],
        cut[2],
        cut[1],
        jnp.where(left, cut[4], other[6]),
        jnp.where(left, other[4], other[5]),
        jnp.where(left, other[5], jnp.where(even, cut[6], other[7])),
        cut[3],
        jnp.where(left, jnp.where(even, cut[7], other[6]), cut[7]),
    ]
    for m, v in enumerate(order):
        line[:, m * block : (m + 1) * block] = v


def first_kernel(staged, spread, *refs):
    me, x, core = position()
    if staged:
        *pieces, codes, stats, strip, whole, gram = refs
        block = pieces[0].shape[0]
        order_codes(spread, codes, block)
        row = 0
        for piece in pieces:
            whole[row : row + piece.shape[0], :] = piece[...]
            row += piece.shape[0]
        first_row = x * (block // 2)
    else:
        whole, stats, strip, gram = refs
        codes, block = spread, strip.shape[0] * 2
        first_row = me * block + x * (block // 2)
    total, width = whole.shape
    mine = pl.ds(pl.multiple_of(first_row, block // 2), block // 2)

    def tile(cols, size, slot=0):
        part = gram.at[slot, :, 0:size]
        part[...] = times(whole[...], whole[cols, :])
        hide_diagonal(part, cols)
        strip[:, cols] = part[mine, :]
        best, sums = columns(part, total, bases_of(codes[:, cols], width))
        stats[0:1, cols] = best
        for level in range(CODES):
            stats[1 + level : 2 + level, cols] = sums[level]
        stats[1 + CODES :, cols] = jnp.zeros((stats.shape[0] - 1 - CODES, size), jnp.float32)

    if staged:
        for slot, (start, size) in enumerate(tiles(total)):
            tile(pl.ds(start, size), size, slot)
    else:

        @pl.loop(0, total // TILE)
        def _(i):
            tile(at(i, TILE), TILE)


def swapped(a, block):
    left, right = a[:, -3 * block : -2 * block], a[:, -block:]
    half = block // 2
    low = lax.broadcasted_iota(jnp.int32, left.shape, 1) < half
    return jnp.where(low, left, pltpu.roll(right, half, 1)), jnp.where(
        low, pltpu.roll(left, half, 1), right
    )


def add_rows(codes, early, late, before, stats, strip, wide, square):
    tail, width = late.shape
    head, block = before.shape[1], 2 * strip.shape[0]
    last = slice(head, head + tail)
    row = 0
    for part in early:
        wide[:, row : row + part.shape[0]] = times(late[...], part[...])
        row += part.shape[0]
    gram = times(late[...], late[...])
    lines, lanes = (lax.broadcasted_iota(jnp.int32, gram.shape, axis) for axis in (0, 1))
    wide[:, last] = jnp.where(lines == lanes, NEG, gram)
    square[...] = jnp.broadcast_to(codes[:, last], (8, tail)).astype(jnp.float32).T
    for row in range(0, tail, 32):
        rows = slice(row, row + 32)
        bases = bases_of(square[rows, 0:1], width)
        best = jnp.full((32, 128), NEG, jnp.float32)
        for col in range(0, head + tail, 128):
            best = jnp.maximum(best, wide[rows, col : col + 128])
        best = jnp.max(best, axis=1, keepdims=True)
        sums = (jnp.zeros((32, 128), jnp.float32),) * CODES
        for col in range(0, head + tail, 128):
            part = powers(wide[rows, col : col + 128] - best, *bases)
            sums = tuple(s + v for s, v in zip(sums, part))
        square[rows, 0:1] = best
        for level in range(CODES):
            square[rows, 1 + level : 2 + level] = jnp.sum(sums[level], axis=1, keepdims=True)
    stats[:, last] = square[...].T
    for start, size in tiles(head):
        cols = pl.ds(start, size)
        bases = bases_of(codes[:, cols], width)
        best, sums = columns(wide.at[:, cols], tail, bases)
        top = jnp.maximum(best, before[0:1, cols])
        was, now = powers(before[0:1, cols] - top, *bases), powers(best - top, *bases)
        stats[0:1, cols] = top
        for level in range(CODES):
            stats[1 + level : 2 + level, cols] = (
                before[1 + level : 2 + level, cols] * was[level] + sums[level] * now[level]
            )
    _, x, _ = position()
    turned = wide[:, 0:block].T
    strip[:, last] = jnp.where(x == 0, turned[: block // 2], turned[block // 2 :])


def second_kernel(
    codes, early, before, part_strip, level_index, fa, fb, ga, stats, strip, whole, level, wide, square
):
    _, x, core = position()
    head, half = early.shape[0], ga.shape[0]
    late = whole.at[head:, :]
    late[spot(core, half), :] = fa[0:half, :]
    late[spot(1 - core, half), :] = fb[0:half, :]
    late[2 * half : 3 * half, :] = fb[half : 2 * half, :]
    late[3 * half : 4 * half, :] = ga[...]
    whole[0:head, :] = early[...]
    strip[:, 0:head] = part_strip[...]
    add_rows(codes, [early], late, before, stats, strip, wide, square)
    stats[1 + CODES :, :] = jnp.zeros((stats.shape[0] - 1 - CODES, stats.shape[1]), jnp.float32)
    theirs = jnp.where(
        core == 0, fa[half : half + 1, 0:1], fb[2 * half : 2 * half + 1, 0:1]
    ).astype(jnp.float32)
    row = lax.broadcasted_iota(jnp.int32, level.shape, 0)
    level[...] = jnp.where(row == 0, level_index[0].astype(jnp.float32), theirs)


def third_kernel(codes, early, before, part_strip, late, _, stats, strip, wide, square):
    strip[:, 0 : early.shape[0]] = part_strip[...]
    add_rows(codes, [early], late, before, stats, strip, wide, square)
    stats[1 + CODES :, :] = jnp.zeros((stats.shape[0] - 1 - CODES, stats.shape[1]), jnp.float32)


def last_kernel(codes, early, middle, before, part_strip, late, keep, send, strip, wide, square):
    _, x, core = position()
    block = late.shape[0]
    half = block // 4
    strip[:, 0 : before.shape[1]] = part_strip[...]
    stats = keep.at[half:, :]
    add_rows(codes, [early, middle], late, before, stats, strip, wide, square)
    stats[1 + CODES :, :] = jnp.zeros((stats.shape[0] - 1 - CODES, stats.shape[1]), jnp.float32)
    keep[0:half, :] = strip[spot(core, half), :]
    send[0:half, :] = strip[spot(1 - core, half), :]
    send[half:, :] = stats[...]
    left, right = swapped(send, block)
    send[:, -3 * block : -2 * block] = left
    send[:, -block:] = right


def counted(*levels):
    row = lax.broadcasted_iota(jnp.int32, (8, 1), 0).astype(jnp.float32) - 1.0
    found = [ref[i : i + 1, 0:1] for ref in levels for i in (0, 1)]
    return sum(jnp.where(row == level, 1.0, 0.0) for level in found)


class Half:
    def __init__(self, own, width, codes, box, count, turned):
        _, x, core = position()
        rows = box.shape[0] - 8
        self.codes, self.width, self.count = codes, width, count
        self.gram, self.stats = box.at[0:rows, :], box.at[rows : rows + 8, :]
        own = spot(own, 4 * rows)
        beta, weight, stats = self.lines(own)
        row = lax.broadcasted_iota(jnp.int32, stats.shape, 0)
        inner = (row > 0) & (row <= CODES)
        lse = jnp.where(inner, count * (beta * stats[0:1] + jnp.log(stats)), 0.0)
        lse = jnp.sum(lse, axis=0, keepdims=True)
        turned[0] = jnp.where(inner, weight, jnp.where(row == 0, stats, lse)).T
        turned[1] = (beta * LOG2E).T
        mine = spot(2 * x + core, rows)
        lead, base = turned[0, mine, :], turned[1, mine, :]
        self.top, self.lse = lead[:, 0:1], lead[:, 7:8]
        self.weight = [lead[:, 1 + c : 2 + c] for c in range(CODES)]
        self.bases = base[:, 6:7], base[:, 5:6]

    def lines(self, cols):
        stats = self.stats[:, cols]
        row = lax.broadcasted_iota(jnp.int32, stats.shape, 0)
        code = self.codes[:, cols].astype(jnp.float32)
        beta = jnp.exp2(0.5 * (code - (row.astype(jnp.float32) - 1.0))) / jnp.sqrt(
            jnp.float32(self.width)
        )
        stats = jnp.where((row > CODES), 1.0, stats)
        return beta, self.count * beta / jnp.where(row == 0, 1.0, stats), stats

    def part(self, cols):
        gram = self.gram[:, cols]
        beta, weight, stats = self.lines(cols)
        by_row = sum(v * w for v, w in zip(powers(gram - self.top, *self.bases), self.weight))
        e = powers(gram - stats[0:1], beta[6:7] * LOG2E, beta[5:6] * LOG2E)
        by_col = sum(v * weight[1 + c : 2 + c] for c, v in enumerate(e))
        return by_row, by_row + by_col


def product(a, b):
    return jnp.dot(a, b, preferred_element_type=jnp.float32)


def store_loss(gap, difference, out):
    out[...] = jnp.broadcast_to(gap + difference, (gap.shape[0], 128)).T[0:1, :]


def half_kernel(width, codes, keep, level, their_level, by_row, both, lse, turned):
    half = Half(0, width, codes, keep, counted(level, their_level), turned)
    for col in range(0, codes.shape[1], 128):
        cols = pl.ds(col, 128)
        by_row[:, cols], both[:, cols] = half.part(cols)
    lse[...] = jnp.broadcast_to(half.lse, lse.shape)


def mix_kernel(
    codes, keep, recv, level, their_level, by_row, both, lse, early, middle, late, sooner, later,
    out, loss, turned, mix
):
    half = Half(0, out.shape[1], codes, recv, counted(level, their_level), turned)
    student = position()[2] == 1
    sign = jnp.where(student, 1.0, -1.0)
    rows = by_row.shape[0]
    gap = jnp.zeros((rows, 128), jnp.float32)
    for col in range(0, codes.shape[1], 128):
        cols = pl.ds(col, 128)
        their_row, their_both = half.part(cols)
        mix[:, cols] = ((WEIGHT * sign) * (both[:, cols] - their_both)).astype(jnp.bfloat16)
        p_row = jnp.where(student, their_row, by_row[:, cols])
        gap = gap + p_row * (recv[0:rows, cols] - keep[0:rows, cols])
    gap = jnp.sum(gap, axis=1, keepdims=True)
    store_loss(sign * gap, sign * (lse[:, 0:1] - half.lse), loss)

    def against(*parts):
        row, total = 0, None
        for part in parts:
            term = product(mix[:, row : row + part.shape[0]], part[...])
            row, total = row + part.shape[0], term if total is None else total + term
        out[...] = total

    @pl.when(student)
    def _():
        against(early, middle, late)

    @pl.when(jnp.logical_not(student))
    def _():
        against(sooner, later)


def wide_mix_kernel(codes, s_box, t_box, level, their_level, student, out, loss, turned):
    total, width = student.shape
    own, count = lax.axis_index("batch"), counted(level, their_level)
    s = Half(own, width, codes, s_box, count, turned.at[0:2])
    t = Half(own, width, codes, t_box, count, turned.at[2:4])
    span, rows = min(SPAN, total), out.shape[0]

    def step(i, carry):
        cols = at(i, span)
        (_, q), (p_row, p) = s.part(cols), t.part(cols)
        gap = jnp.sum(p_row * (t_box[0:rows, cols] - s_box[0:rows, cols]), axis=1, keepdims=True)
        mix = (WEIGHT * (q - p)).astype(jnp.bfloat16)
        return carry[0] + product(mix, student[cols, :]), carry[1] + gap

    zero = jnp.zeros((rows, width), jnp.float32), jnp.zeros((rows, 1), jnp.float32)
    out[...], gap = lax.fori_loop(0, total // span, step, zero)
    store_loss(gap, s.lse - t.lse, loss)


def call(kernel, shapes, scratch, limit, *args):
    return pl.pallas_call(
        kernel,
        out_shape=shapes,
        in_specs=[SMEM if a.shape == (1,) else VMEM for a in args],
        out_specs=[VMEM] * len(shapes),
        scratch_shapes=scratch,
        compiler_params=pltpu.CompilerParams(vmem_limit_bytes=limit << 20),
    )(*args)


def room(rows, cols):
    return [pltpu.VMEM((rows, cols), jnp.float32), pltpu.VMEM((rows, 8), jnp.float32)]


def join(parts, *behind):
    def kernel(*refs):
        row = 0
        for part in refs[: len(parts)]:
            refs[-1][row : row + part.shape[0], :] = part[...]
            row += part.shape[0]

    dims = sum(p.shape[0] for p in parts), parts[0].shape[1]
    return call(kernel, [shape(*dims, dtype=parts[0].dtype)], [], 16, *parts, *behind)[0]


def shape(*dims, dtype=jnp.float32):
    return jax.ShapeDtypeStruct(dims, dtype)


def shards(mesh, embeddings, spread_code, level_index):
    block, width = embeddings.shape[1:]
    batches, parts = mesh.shape["batch"], mesh.shape["temp"]
    total = block * batches
    me, part = lax.axis_index("batch"), lax.axis_index("temp")
    x, core = part // 2, part % 2
    rows, half = block // 2, block // 4

    def send(a, to):
        pairs = []
        for b in range(batches):
            for t in range(parts):
                there = to(b, t // 2, t % 2)
                pairs.append((b * parts + t, there[0] * parts + there[1] * 2 + there[2]))
        return lax.ppermute(a, ALL, pairs)

    over_core = lambda b, x, c: (b, x, 1 - c)
    over_x = lambda b, x, c: (b, 1 - x, c)
    u = lax.dynamic_index_in_dim(embeddings, core, 0, keepdims=False)
    out_shapes = [shape(half, width), shape(1, half)]
    codes = spread_code[None, :]

    if batches != 8 or parts != 4:
        whole = lax.all_gather(u, "batch", axis=0, tiled=True)
        theirs = send(level_index, over_x)
        stats, strip = call(
            functools.partial(first_kernel, False),
            [shape(8, total), shape(rows, total)],
            [pltpu.VMEM((1, total, TILE), jnp.float32)],
            56,
            codes,
            whole,
        )
        level = jnp.stack([level_index, theirs] + [theirs] * 6).astype(jnp.float32)
        level = jnp.broadcast_to(level, (8, 128))
        share = lambda c: lax.dynamic_slice_in_dim(strip, c * half, half)
        keep = jnp.concatenate([share(core), stats])
        recv = send(jnp.concatenate([share(1 - core), stats]), over_core)
        student = jnp.where(core == 1, whole, send(whole, over_core))
        out, loss = call(
            wide_mix_kernel,
            out_shapes,
            [pltpu.VMEM((4, block, 8), jnp.float32)],
            56,
            codes,
            jnp.where(core == 1, keep, recv),
            jnp.where(core == 1, recv, keep),
            level,
            send(level, over_core),
            student,
        )
        return out, loss[0]

    near = lambda b, x, c: (b ^ 2, x, c)
    far = lambda b, x, c: (b ^ 4, x, c)
    over_y = lambda b, x, c: (b ^ 1, x, c)
    turn = lambda b, x, c: (over_y if c else over_x)(b, x, c)
    return_turn = lambda b, x, c: (over_x if c else over_y)(b, x, c)
    level = jnp.broadcast_to(level_index.astype(jnp.bfloat16), (16, width))
    f = send(lax.dynamic_slice_in_dim(u, x * rows, rows, 0), far)
    n = send(u, near)
    y = send(u, over_y)
    g = send(f, near)
    ny = send(join([y], g), near)
    fa = send(join([f, level]), turn)
    fb = send(join([f, fa[:rows], level], g), return_turn)
    ga = send(g, turn)
    sooner = send(join([join([u, n]), y, f, g], fa), over_core)
    some, head = 4 * block, 6 * block
    codes, a_stats, a_strip, a_rows = call(
        functools.partial(first_kernel, True),
        [
            shape(1, total, dtype=jnp.int32),
            shape(8, some),
            shape(rows, some),
            shape(some, width, dtype=jnp.bfloat16),
        ],
        [pltpu.VMEM((some // TILE, some, TILE), jnp.float32)],
        16,
        codes,
        u,
        n,
        y,
        f,
        g,
    )
    gb = send(join([g, ga], sooner, a_stats), return_turn)
    b_stats, b_strip, b_rows, levels = call(
        second_kernel,
        [
            shape(8, head),
            shape(rows, head),
            shape(head, width, dtype=jnp.bfloat16),
            shape(8, 128),
        ],
        room(head - some, head),
        16,
        codes,
        a_rows,
        a_stats,
        a_strip,
        level_index,
        fa,
        fb,
        ga,
    )
    their_levels = send(levels, over_core)
    c_stats, c_strip = call(
        third_kernel,
        [shape(8, total - block), shape(rows, total - block)],
        room(block, total - block),
        16,
        codes,
        b_rows,
        b_stats,
        b_strip,
        ny,
        their_levels,
    )
    later = send(
        join([b_rows[some : some + 3 * rows], gb[:rows], ny, ga, gb[rows:]], c_stats), over_core
    )
    keep, mail = call(
        last_kernel,
        [shape(half + 8, total), shape(half + 8, total)],
        [pltpu.VMEM((rows, total), jnp.float32)] + room(block, total),
        16,
        codes,
        b_rows,
        ny,
        c_stats,
        c_strip,
        gb,
    )
    recv = send(mail, over_core)
    by_row, both, lse = call(
        functools.partial(half_kernel, width),
        [shape(half, total), shape(half, total), shape(half, 8)],
        [pltpu.VMEM((2, block, 8), jnp.float32)],
        16,
        codes,
        keep,
        levels,
        their_levels,
    )
    out, loss = call(
        mix_kernel,
        out_shapes,
        [pltpu.VMEM((2, block, 8), jnp.float32), pltpu.VMEM((half, total), jnp.bfloat16)],
        16,
        codes,
        keep,
        recv,
        levels,
        their_levels,
        by_row,
        both,
        lse,
        b_rows,
        ny,
        gb,
        sooner,
        later,
    )
    return out, loss[0]


def solution(mesh):
    in_specs = (P(None, "batch", None), P(), P("temp"))
    out_specs = (P(("batch", "temp"), None), P(("batch", "temp")))
    return jax.shard_map(
        functools.partial(shards, mesh),
        mesh=mesh,
        in_specs=in_specs,
        out_specs=out_specs,
        check_vma=False,
    )
```

```python
import functools

import jax
import jax.numpy as jnp
from jax import lax
from jax.experimental import pallas as pl
from jax.experimental.pallas import tpu as pltpu
from jax.sharding import PartitionSpec as P

WEIGHT = 16.0
NEG = -1e30
LOG2E = 1.4426950408889634
CODES = 6
TILE = 256
CHUNK = 128
SPAN = 1024
ALL = ("batch", "temp")
SMEM = pl.BlockSpec(memory_space=pltpu.SMEM)
VMEM = pl.BlockSpec(memory_space=pltpu.VMEM)


def carried(count, body, carry):
    if count <= 8:
        for i in range(count):
            carry = body(i, carry)
        return carry
    return lax.fori_loop(0, count, body, carry)


def at(i, size):
    return pl.ds(i * size if isinstance(i, int) else pl.multiple_of(i * size, size), size)


def widths(code, width):
    root = jnp.sqrt(jnp.float32(width))
    return [jnp.exp2(0.5 * (code - jnp.float32(level))) / root for level in range(CODES)]


def powers(d, widest, wide):
    e = [None] * CODES
    e[5], e[4] = jnp.exp2(d * widest), jnp.exp2(d * wide)
    for level in (3, 2, 1, 0):
        e[level] = e[level + 2] * e[level + 2]
    return e


def columns(gram, count, bases):
    size = min(CHUNK, count)
    tile = gram.shape[1]

    def lines(i):
        for j in range(0, size, 8):
            start = i * size + j
            yield gram[pl.ds(start if isinstance(i, int) else pl.multiple_of(start, 8), 8), :]

    def top(i, best):
        for line in lines(i):
            best = jnp.maximum(best, line)
        return best

    best = carried(count // size, top, jnp.full((8, tile), NEG, jnp.float32))
    best = jnp.max(best, axis=0, keepdims=True)

    def add(i, sums):
        for line in lines(i):
            sums = tuple(s + v for s, v in zip(sums, powers(line - best, *bases)))
        return sums

    sums = carried(count // size, add, (jnp.zeros((8, tile), jnp.float32),) * CODES)
    return best, [jnp.sum(s, axis=0, keepdims=True) for s in sums]


def times(a, b):
    return lax.dot_general(a, b, (((1,), (1,)), ((), ())), preferred_element_type=jnp.float32)


def hide_diagonal(gram, rows):
    square = gram[rows, :]
    own = lax.broadcasted_iota(jnp.int32, square.shape, 0) == lax.broadcasted_iota(
        jnp.int32, square.shape, 1
    )
    gram[rows, :] = jnp.where(own, NEG, square)


def bases_of(code, width):
    beta = widths(code.astype(jnp.float32), width)
    return beta[5] * LOG2E, beta[4] * LOG2E


def tiles(total):
    return [(i, min(TILE, total - i)) for i in range(0, total, TILE)]


def position():
    part = lax.axis_index("temp")
    return lax.axis_index("batch"), part // 2, part % 2


def spot(i, size):
    return pl.ds(pl.multiple_of(i * size, size), size)


def order_codes(spread, line, block):
    me, x, core = position()
    half = block // 2
    cut = [spread[:, spot(me ^ m, block)] for m in range(8)]
    cut[4:] = [jnp.where(x == 0, v, pltpu.roll(v, half, 1)) for v in cut[4:]]
    left = lax.broadcasted_iota(jnp.int32, cut[0].shape, 1) < half
    other = [None] * 4 + [pltpu.roll(v, half, 1) for v in cut[4:]]
    even = core == 0
    order = [
        cut[0],
        cut[2],
        cut[1],
        jnp.where(left, cut[4], other[6]),
        jnp.where(left, other[4], other[5]),
        jnp.where(left, other[5], jnp.where(even, cut[6], other[7])),
        cut[3],
        jnp.where(left, jnp.where(even, cut[7], other[6]), cut[7]),
    ]
    for m, v in enumerate(order):
        line[:, m * block : (m + 1) * block] = v


def first_kernel(staged, spread, *refs):
    me, x, core = position()
    if staged:
        *pieces, codes, stats, strip, whole, gram = refs
        block = pieces[0].shape[0]
        order_codes(spread, codes, block)
        row = 0
        for piece in pieces:
            whole[row : row + piece.shape[0], :] = piece[...]
            row += piece.shape[0]
        first_row = x * (block // 2)
    else:
        whole, stats, strip, gram = refs
        codes, block = spread, strip.shape[0] * 2
        first_row = me * block + x * (block // 2)
    total, width = whole.shape
    mine = pl.ds(pl.multiple_of(first_row, block // 2), block // 2)

    def tile(cols, size, slot=0):
        part = gram.at[slot, :, 0:size]
        part[...] = times(whole[...], whole[cols, :])
        hide_diagonal(part, cols)
        strip[:, cols] = part[mine, :]
        best, sums = columns(part, total, bases_of(codes[:, cols], width))
        stats[0:1, cols] = best
        for level in range(CODES):
            stats[1 + level : 2 + level, cols] = sums[level]
        stats[1 + CODES :, cols] = jnp.zeros((stats.shape[0] - 1 - CODES, size), jnp.float32)

    if staged:
        for slot, (start, size) in enumerate(tiles(total)):
            tile(pl.ds(start, size), size, slot)
    else:

        @pl.loop(0, total // TILE)
        def _(i):
            tile(at(i, TILE), TILE)


def swapped(a, block):
    left, right = a[:, -3 * block : -2 * block], a[:, -block:]
    half = block // 2
    low = lax.broadcasted_iota(jnp.int32, left.shape, 1) < half
    return jnp.where(low, left, pltpu.roll(right, half, 1)), jnp.where(
        low, pltpu.roll(left, half, 1), right
    )


def add_rows(codes, early, late, before, stats, strip, wide, square):
    tail, width = late.shape
    head, block = before.shape[1], 2 * strip.shape[0]
    last = slice(head, head + tail)
    row = 0
    for part in early:
        wide[:, row : row + part.shape[0]] = times(late[...], part[...])
        row += part.shape[0]
    gram = times(late[...], late[...])
    lines, lanes = (lax.broadcasted_iota(jnp.int32, gram.shape, axis) for axis in (0, 1))
    wide[:, last] = jnp.where(lines == lanes, NEG, gram)
    square[...] = jnp.broadcast_to(codes[:, last], (8, tail)).astype(jnp.float32).T
    for row in range(0, tail, 32):
        rows = slice(row, row + 32)
        bases = bases_of(square[rows, 0:1], width)
        best = jnp.full((32, 128), NEG, jnp.float32)
        for col in range(0, head + tail, 128):
            best = jnp.maximum(best, wide[rows, col : col + 128])
        best = jnp.max(best, axis=1, keepdims=True)
        sums = (jnp.zeros((32, 128), jnp.float32),) * CODES
        for col in range(0, head + tail, 128):
            part = powers(wide[rows, col : col + 128] - best, *bases)
            sums = tuple(s + v for s, v in zip(sums, part))
        square[rows, 0:1] = best
        for level in range(CODES):
            square[rows, 1 + level : 2 + level] = jnp.sum(sums[level], axis=1, keepdims=True)
    stats[:, last] = square[...].T
    for start, size in tiles(head):
        cols = pl.ds(start, size)
        bases = bases_of(codes[:, cols], width)
        best, sums = columns(wide.at[:, cols], tail, bases)
        top = jnp.maximum(best, before[0:1, cols])
        was, now = powers(before[0:1, cols] - top, *bases), powers(best - top, *bases)
        stats[0:1, cols] = top
        for level in range(CODES):
            stats[1 + level : 2 + level, cols] = (
                before[1 + level : 2 + level, cols] * was[level] + sums[level] * now[level]
            )
    _, x, _ = position()
    turned = wide[:, 0:block].T
    strip[:, last] = jnp.where(x == 0, turned[: block // 2], turned[block // 2 :])


def second_kernel(
    codes, early, before, part_strip, level_index, fa, fb, ga, stats, strip, whole, level, wide, square
):
    _, x, core = position()
    head, half = early.shape[0], ga.shape[0]
    late = whole.at[head:, :]
    late[spot(core, half), :] = fa[0:half, :]
    late[spot(1 - core, half), :] = fb[0:half, :]
    late[2 * half : 3 * half, :] = fb[half : 2 * half, :]
    late[3 * half : 4 * half, :] = ga[...]
    whole[0:head, :] = early[...]
    strip[:, 0:head] = part_strip[...]
    add_rows(codes, [early], late, before, stats, strip, wide, square)
    stats[1 + CODES :, :] = jnp.zeros((stats.shape[0] - 1 - CODES, stats.shape[1]), jnp.float32)
    theirs = jnp.where(
        core == 0, fa[half : half + 16, 0:128], fb[2 * half : 2 * half + 16, 0:128]
    ).astype(jnp.float32)[0:1, 0:1]
    row = lax.broadcasted_iota(jnp.int32, level.shape, 0)
    level[...] = jnp.where(row == 0, level_index[0].astype(jnp.float32), theirs)


def third_kernel(codes, early, before, part_strip, late, _, stats, strip, wide, square):
    strip[:, 0 : early.shape[0]] = part_strip[...]
    add_rows(codes, [early], late, before, stats, strip, wide, square)
    stats[1 + CODES :, :] = jnp.zeros((stats.shape[0] - 1 - CODES, stats.shape[1]), jnp.float32)


def last_kernel(codes, early, middle, before, part_strip, late, keep, send, strip, wide, square):
    _, x, core = position()
    block = late.shape[0]
    half = block // 4
    strip[:, 0 : before.shape[1]] = part_strip[...]
    stats = keep.at[half:, :]
    add_rows(codes, [early, middle], late, before, stats, strip, wide, square)
    stats[1 + CODES :, :] = jnp.zeros((stats.shape[0] - 1 - CODES, stats.shape[1]), jnp.float32)
    keep[0:half, :] = strip[spot(core, half), :]
    send[0:half, :] = strip[spot(1 - core, half), :]
    send[half:, :] = stats[...]
    left, right = swapped(send, block)
    send[:, -3 * block : -2 * block] = left
    send[:, -block:] = right


def counted(*levels):
    row = lax.broadcasted_iota(jnp.int32, (8, 1), 0).astype(jnp.float32) - 1.0
    found = [ref[i : i + 1, 0:1] for ref in levels for i in (0, 1)]
    return sum(jnp.where(row == level, 1.0, 0.0) for level in found)


class Half:
    def __init__(self, own, width, codes, box, count, turned):
        _, x, core = position()
        rows = box.shape[0] - 8
        self.codes, self.width, self.count = codes, width, count
        self.gram, self.stats = box.at[0:rows, :], box.at[rows : rows + 8, :]
        own = spot(own, 4 * rows)
        beta, weight, stats = self.lines(own)
        row = lax.broadcasted_iota(jnp.int32, stats.shape, 0)
        inner = (row > 0) & (row <= CODES)
        lse = jnp.where(inner, count * (beta * stats[0:1] + jnp.log(stats)), 0.0)
        lse = jnp.sum(lse, axis=0, keepdims=True)
        turned[0] = jnp.where(inner, weight, jnp.where(row == 0, stats, lse)).T
        turned[1] = (beta * LOG2E).T
        mine = spot(2 * x + core, rows)
        lead, base = turned[0, mine, :], turned[1, mine, :]
        self.top, self.lse = lead[:, 0:1], lead[:, 7:8]
        self.weight = [lead[:, 1 + c : 2 + c] for c in range(CODES)]
        self.bases = base[:, 6:7], base[:, 5:6]

    def lines(self, cols):
        stats = self.stats[:, cols]
        row = lax.broadcasted_iota(jnp.int32, stats.shape, 0)
        code = self.codes[:, cols].astype(jnp.float32)
        beta = jnp.exp2(0.5 * (code - (row.astype(jnp.float32) - 1.0))) / jnp.sqrt(
            jnp.float32(self.width)
        )
        stats = jnp.where((row > CODES), 1.0, stats)
        return beta, self.count * beta / jnp.where(row == 0, 1.0, stats), stats

    def part(self, cols):
        gram = self.gram[:, cols]
        beta, weight, stats = self.lines(cols)
        by_row = sum(v * w for v, w in zip(powers(gram - self.top, *self.bases), self.weight))
        e = powers(gram - stats[0:1], beta[6:7] * LOG2E, beta[5:6] * LOG2E)
        by_col = sum(v * weight[1 + c : 2 + c] for c, v in enumerate(e))
        return by_row, by_row + by_col


def product(a, b):
    return jnp.dot(a, b, preferred_element_type=jnp.float32)


def store_loss(gap, difference, out):
    out[...] = jnp.broadcast_to(gap + difference, (gap.shape[0], 128)).T[0:1, :]


def half_kernel(width, codes, keep, level, their_level, by_row, both, lse, turned):
    half = Half(0, width, codes, keep, counted(level, their_level), turned)
    for col in range(0, codes.shape[1], 128):
        cols = pl.ds(col, 128)
        by_row[:, cols], both[:, cols] = half.part(cols)
    lse[...] = jnp.broadcast_to(half.lse, lse.shape)


def mix_kernel(
    codes, keep, recv, level, their_level, by_row, both, lse, early, middle, late, sooner, later,
    out, loss, turned, mix
):
    half = Half(0, out.shape[1], codes, recv, counted(level, their_level), turned)
    student = position()[2] == 1
    sign = jnp.where(student, 1.0, -1.0)
    rows = by_row.shape[0]
    gap = jnp.zeros((rows, 128), jnp.float32)
    for col in range(0, codes.shape[1], 128):
        cols = pl.ds(col, 128)
        their_row, their_both = half.part(cols)
        mix[:, cols] = ((WEIGHT * sign) * (both[:, cols] - their_both)).astype(jnp.bfloat16)
        p_row = jnp.where(student, their_row, by_row[:, cols])
        gap = gap + p_row * (recv[0:rows, cols] - keep[0:rows, cols])
    gap = jnp.sum(gap, axis=1, keepdims=True)
    store_loss(sign * gap, sign * (lse[:, 0:1] - half.lse), loss)

    def against(*parts):
        row, total = 0, None
        for part in parts:
            term = product(mix[:, row : row + part.shape[0]], part[...])
            row, total = row + part.shape[0], term if total is None else total + term
        out[...] = total

    @pl.when(student)
    def _():
        against(early, middle, late)

    @pl.when(jnp.logical_not(student))
    def _():
        against(sooner, later)


def wide_mix_kernel(codes, s_box, t_box, level, their_level, student, out, loss, turned):
    total, width = student.shape
    own, count = lax.axis_index("batch"), counted(level, their_level)
    s = Half(own, width, codes, s_box, count, turned.at[0:2])
    t = Half(own, width, codes, t_box, count, turned.at[2:4])
    span, rows = min(SPAN, total), out.shape[0]

    def step(i, carry):
        cols = at(i, span)
        (_, q), (p_row, p) = s.part(cols), t.part(cols)
        gap = jnp.sum(p_row * (t_box[0:rows, cols] - s_box[0:rows, cols]), axis=1, keepdims=True)
        mix = (WEIGHT * (q - p)).astype(jnp.bfloat16)
        return carry[0] + product(mix, student[cols, :]), carry[1] + gap

    zero = jnp.zeros((rows, width), jnp.float32), jnp.zeros((rows, 1), jnp.float32)
    out[...], gap = lax.fori_loop(0, total // span, step, zero)
    store_loss(gap, s.lse - t.lse, loss)


def call(kernel, shapes, scratch, limit, *args):
    return pl.pallas_call(
        kernel,
        out_shape=shapes,
        in_specs=[SMEM if a.shape == (1,) else VMEM for a in args],
        out_specs=[VMEM] * len(shapes),
        scratch_shapes=scratch,
        compiler_params=pltpu.CompilerParams(vmem_limit_bytes=limit << 20),
    )(*args)


def room(rows, cols):
    return [pltpu.VMEM((rows, cols), jnp.float32), pltpu.VMEM((rows, 8), jnp.float32)]


def join(parts, *behind):
    def kernel(*refs):
        row = 0
        for part in refs[: len(parts)]:
            refs[-1][row : row + part.shape[0], :] = part[...]
            row += part.shape[0]

    dims = sum(p.shape[0] for p in parts), parts[0].shape[1]
    return call(kernel, [shape(*dims, dtype=parts[0].dtype)], [], 16, *parts, *behind)[0]


def shape(*dims, dtype=jnp.float32):
    return jax.ShapeDtypeStruct(dims, dtype)


def shards(mesh, embeddings, spread_code, level_index):
    block, width = embeddings.shape[1:]
    batches, parts = mesh.shape["batch"], mesh.shape["temp"]
    total = block * batches
    me, part = lax.axis_index("batch"), lax.axis_index("temp")
    x, core = part // 2, part % 2
    rows, half = block // 2, block // 4

    def send(a, to):
        pairs = []
        for b in range(batches):
            for t in range(parts):
                there = to(b, t // 2, t % 2)
                pairs.append((b * parts + t, there[0] * parts + there[1] * 2 + there[2]))
        return lax.ppermute(a, ALL, pairs)

    over_core = lambda b, x, c: (b, x, 1 - c)
    over_x = lambda b, x, c: (b, 1 - x, c)
    u = lax.dynamic_index_in_dim(embeddings, core, 0, keepdims=False)
    out_shapes = [shape(half, width), shape(1, half)]
    codes = spread_code[None, :]

    if batches != 8 or parts != 4:
        whole = lax.all_gather(u, "batch", axis=0, tiled=True)
        theirs = send(level_index, over_x)
        stats, strip = call(
            functools.partial(first_kernel, False),
            [shape(8, total), shape(rows, total)],
            [pltpu.VMEM((1, total, TILE), jnp.float32)],
            56,
            codes,
            whole,
        )
        level = jnp.stack([level_index, theirs] + [theirs] * 6).astype(jnp.float32)
        level = jnp.broadcast_to(level, (8, 128))
        share = lambda c: lax.dynamic_slice_in_dim(strip, c * half, half)
        keep = jnp.concatenate([share(core), stats])
        recv = send(jnp.concatenate([share(1 - core), stats]), over_core)
        student = jnp.where(core == 1, whole, send(whole, over_core))
        out, loss = call(
            wide_mix_kernel,
            out_shapes,
            [pltpu.VMEM((4, block, 8), jnp.float32)],
            56,
            codes,
            jnp.where(core == 1, keep, recv),
            jnp.where(core == 1, recv, keep),
            level,
            send(level, over_core),
            student,
        )
        return out, loss[0]

    near = lambda b, x, c: (b ^ 2, x, c)
    far = lambda b, x, c: (b ^ 4, x, c)
    over_y = lambda b, x, c: (b ^ 1, x, c)
    turn = lambda b, x, c: (over_y if c else over_x)(b, x, c)
    return_turn = lambda b, x, c: (over_x if c else over_y)(b, x, c)
    level = jnp.broadcast_to(level_index.astype(jnp.bfloat16), (16, width))
    f = send(lax.dynamic_slice_in_dim(u, x * rows, rows, 0), far)
    n = send(u, near)
    y = send(u, over_y)
    g = send(f, near)
    ny = send(join([y], g), near)
    fa = send(join([f, level]), turn)
    fb = send(join([f, fa[:rows], level], g), return_turn)
    ga = send(g, turn)
    sooner = send(join([join([u, n]), y, f, g], fa), over_core)
    some, head = 4 * block, 6 * block
    codes, a_stats, a_strip, a_rows = call(
        functools.partial(first_kernel, True),
        [
            shape(1, total, dtype=jnp.int32),
            shape(8, some),
            shape(rows, some),
            shape(some, width, dtype=jnp.bfloat16),
        ],
        [pltpu.VMEM((some // TILE, some, TILE), jnp.float32)],
        16,
        codes,
        u,
        n,
        y,
        f,
        g,
    )
    gb = send(join([g, ga], sooner, a_stats), return_turn)
    b_stats, b_strip, b_rows, levels = call(
        second_kernel,
        [
            shape(8, head),
            shape(rows, head),
            shape(head, width, dtype=jnp.bfloat16),
            shape(8, 128),
        ],
        room(head - some, head),
        16,
        codes,
        a_rows,
        a_stats,
        a_strip,
        level_index,
        fa,
        fb,
        ga,
    )
    their_levels = send(levels, over_core)
    c_stats, c_strip = call(
        third_kernel,
        [shape(8, total - block), shape(rows, total - block)],
        room(block, total - block),
        16,
        codes,
        b_rows,
        b_stats,
        b_strip,
        ny,
        their_levels,
    )
    later = send(
        join([b_rows[some : some + 3 * rows], gb[:rows], ny, ga, gb[rows:]], c_stats), over_core
    )
    keep, mail = call(
        last_kernel,
        [shape(half + 8, total), shape(half + 8, total)],
        [pltpu.VMEM((rows, total), jnp.float32)] + room(block, total),
        16,
        codes,
        b_rows,
        ny,
        c_stats,
        c_strip,
        gb,
    )
    recv = send(mail, over_core)
    by_row, both, lse = call(
        functools.partial(half_kernel, width),
        [shape(half, total), shape(half, total), shape(half, 8)],
        [pltpu.VMEM((2, block, 8), jnp.float32)],
        16,
        codes,
        keep,
        levels,
        their_levels,
    )
    out, loss = call(
        mix_kernel,
        out_shapes,
        [pltpu.VMEM((2, block, 8), jnp.float32), pltpu.VMEM((half, total), jnp.bfloat16)],
        16,
        codes,
        keep,
        recv,
        levels,
        their_levels,
        by_row,
        both,
        lse,
        b_rows,
        ny,
        gb,
        sooner,
        later,
    )
    return out, loss[0]


def solution(mesh):
    in_specs = (P(None, "batch", None), P(), P("temp"))
    out_specs = (P(("batch", "temp"), None), P(("batch", "temp")))
    return jax.shard_map(
        functools.partial(shards, mesh),
        mesh=mesh,
        in_specs=in_specs,
        out_specs=out_specs,
        check_vma=False,
    )
```

```python
import functools

import jax
import jax.numpy as jnp
from jax import lax
from jax.experimental import pallas as pl
from jax.experimental.pallas import tpu as pltpu
from jax.sharding import PartitionSpec as P

WEIGHT = 16.0
NEG = -1e30
LOG2E = 1.4426950408889634
CODES = 6
TILE = 256
CHUNK = 128
SPAN = 1024
ALL = ("batch", "temp")
SMEM = pl.BlockSpec(memory_space=pltpu.SMEM)
VMEM = pl.BlockSpec(memory_space=pltpu.VMEM)


def carried(count, body, carry):
    if count <= 8:
        for i in range(count):
            carry = body(i, carry)
        return carry
    return lax.fori_loop(0, count, body, carry)


def at(i, size):
    return pl.ds(i * size if isinstance(i, int) else pl.multiple_of(i * size, size), size)


def widths(code, width):
    root = jnp.sqrt(jnp.float32(width))
    return [jnp.exp2(0.5 * (code - jnp.float32(level))) / root for level in range(CODES)]


def powers(d, widest, wide):
    e = [None] * CODES
    e[5], e[4] = jnp.exp2(d * widest), jnp.exp2(d * wide)
    for level in (3, 2, 1, 0):
        e[level] = e[level + 2] * e[level + 2]
    return e


def columns(gram, count, bases):
    size = min(CHUNK, count)
    tile = gram.shape[1]

    def lines(i):
        for j in range(0, size, 8):
            start = i * size + j
            yield gram[pl.ds(start if isinstance(i, int) else pl.multiple_of(start, 8), 8), :]

    def top(i, best):
        for line in lines(i):
            best = jnp.maximum(best, line)
        return best

    best = carried(count // size, top, jnp.full((8, tile), NEG, jnp.float32))
    best = jnp.max(best, axis=0, keepdims=True)

    def add(i, sums):
        for line in lines(i):
            sums = tuple(s + v for s, v in zip(sums, powers(line - best, *bases)))
        return sums

    sums = carried(count // size, add, (jnp.zeros((8, tile), jnp.float32),) * CODES)
    return best, [jnp.sum(s, axis=0, keepdims=True) for s in sums]


def times(a, b):
    return lax.dot_general(a, b, (((1,), (1,)), ((), ())), preferred_element_type=jnp.float32)


def hide_diagonal(gram, rows):
    square = gram[rows, :]
    own = lax.broadcasted_iota(jnp.int32, square.shape, 0) == lax.broadcasted_iota(
        jnp.int32, square.shape, 1
    )
    gram[rows, :] = jnp.where(own, NEG, square)


def bases_of(code, width):
    beta = widths(code.astype(jnp.float32), width)
    return beta[5] * LOG2E, beta[4] * LOG2E


def tiles(total):
    return [(i, min(TILE, total - i)) for i in range(0, total, TILE)]


def position():
    part = lax.axis_index("temp")
    return lax.axis_index("batch"), part // 2, part % 2


def spot(i, size):
    return pl.ds(pl.multiple_of(i * size, size), size)


def order_codes(spread, line, block):
    me, x, core = position()
    half = block // 2
    cut = [spread[:, spot(me ^ m, block)] for m in range(8)]
    cut[4:] = [jnp.where(x == 0, v, pltpu.roll(v, half, 1)) for v in cut[4:]]
    left = lax.broadcasted_iota(jnp.int32, cut[0].shape, 1) < half
    other = [None] * 4 + [pltpu.roll(v, half, 1) for v in cut[4:]]
    even = core == 0
    order = [
        cut[0],
        cut[2],
        cut[1],
        jnp.where(left, cut[4], other[6]),
        jnp.where(left, other[4], other[5]),
        jnp.where(left, other[5], jnp.where(even, cut[6], other[7])),
        cut[3],
        jnp.where(left, jnp.where(even, cut[7], other[6]), cut[7]),
    ]
    for m, v in enumerate(order):
        line[:, m * block : (m + 1) * block] = v


def first_kernel(staged, spread, *refs):
    me, x, core = position()
    if staged:
        *pieces, codes, stats, strip, whole, gram = refs
        block = pieces[0].shape[0]
        order_codes(spread, codes, block)
        row = 0
        for piece in pieces:
            whole[row : row + piece.shape[0], :] = piece[...]
            row += piece.shape[0]
        first_row = x * (block // 2)
    else:
        whole, stats, strip, gram = refs
        codes, block = spread, strip.shape[0] * 2
        first_row = me * block + x * (block // 2)
    total, width = whole.shape
    mine = pl.ds(pl.multiple_of(first_row, block // 2), block // 2)

    def tile(cols, size, slot=0):
        part = gram.at[slot, :, 0:size]
        part[...] = times(whole[...], whole[cols, :])
        hide_diagonal(part, cols)
        strip[:, cols] = part[mine, :]
        best, sums = columns(part, total, bases_of(codes[:, cols], width))
        stats[0:1, cols] = best
        for level in range(CODES):
            stats[1 + level : 2 + level, cols] = sums[level]
        stats[1 + CODES :, cols] = jnp.zeros((stats.shape[0] - 1 - CODES, size), jnp.float32)

    if staged:
        for slot, (start, size) in enumerate(tiles(total)):
            tile(pl.ds(start, size), size, slot)
    else:

        @pl.loop(0, total // TILE)
        def _(i):
            tile(at(i, TILE), TILE)


def swapped(a, block):
    left, right = a[:, -3 * block : -2 * block], a[:, -block:]
    half = block // 2
    low = lax.broadcasted_iota(jnp.int32, left.shape, 1) < half
    return jnp.where(low, left, pltpu.roll(right, half, 1)), jnp.where(
        low, pltpu.roll(left, half, 1), right
    )


def add_rows(codes, early, late, before, stats, strip, wide, square):
    tail, width = late.shape
    head, block = before.shape[1], 2 * strip.shape[0]
    last = slice(head, head + tail)
    row = 0
    for part in early:
        wide[:, row : row + part.shape[0]] = times(late[...], part[...])
        row += part.shape[0]
    gram = times(late[...], late[...])
    lines, lanes = (lax.broadcasted_iota(jnp.int32, gram.shape, axis) for axis in (0, 1))
    wide[:, last] = jnp.where(lines == lanes, NEG, gram)
    square[...] = jnp.broadcast_to(codes[:, last], (8, tail)).astype(jnp.float32).T
    for row in range(0, tail, 32):
        rows = slice(row, row + 32)
        bases = bases_of(square[rows, 0:1], width)
        best = jnp.full((32, 128), NEG, jnp.float32)
        for col in range(0, head + tail, 128):
            best = jnp.maximum(best, wide[rows, col : col + 128])
        best = jnp.max(best, axis=1, keepdims=True)
        sums = (jnp.zeros((32, 128), jnp.float32),) * CODES
        for col in range(0, head + tail, 128):
            part = powers(wide[rows, col : col + 128] - best, *bases)
            sums = tuple(s + v for s, v in zip(sums, part))
        square[rows, 0:1] = best
        for level in range(CODES):
            square[rows, 1 + level : 2 + level] = jnp.sum(sums[level], axis=1, keepdims=True)
    stats[:, last] = square[...].T
    for start, size in tiles(head):
        cols = pl.ds(start, size)
        bases = bases_of(codes[:, cols], width)
        best, sums = columns(wide.at[:, cols], tail, bases)
        top = jnp.maximum(best, before[0:1, cols])
        was, now = powers(before[0:1, cols] - top, *bases), powers(best - top, *bases)
        stats[0:1, cols] = top
        for level in range(CODES):
            stats[1 + level : 2 + level, cols] = (
                before[1 + level : 2 + level, cols] * was[level] + sums[level] * now[level]
            )
    _, x, _ = position()
    turned = wide[:, 0:block].T
    strip[:, last] = jnp.where(x == 0, turned[: block // 2], turned[block // 2 :])


def second_kernel(
    codes, early, before, part_strip, level_index, fa, fb, ga, stats, strip, whole, level, wide, square
):
    _, x, core = position()
    head, half = early.shape[0], ga.shape[0]
    late = whole.at[head:, :]
    late[spot(core, half), :] = fa[0:half, :]
    late[spot(1 - core, half), :] = fb[0:half, :]
    late[2 * half : 3 * half, :] = fb[half : 2 * half, :]
    late[3 * half : 4 * half, :] = ga[...]
    whole[0:head, :] = early[...]
    strip[:, 0:head] = part_strip[...]
    add_rows(codes, [early], late, before, stats, strip, wide, square)
    stats[1 + CODES :, :] = jnp.zeros((stats.shape[0] - 1 - CODES, stats.shape[1]), jnp.float32)
    theirs = jnp.where(
        core == 0, fa[half : half + 16, 0:128], fb[2 * half : 2 * half + 16, 0:128]
    ).astype(jnp.float32)[0:1, 0:1]
    share = level.shape[0] - 8
    level[0:share, :] = strip[spot(1 - core, share), 0 : level.shape[1]]
    row = lax.broadcasted_iota(jnp.int32, (8, level.shape[1]), 0)
    level[share:, :] = jnp.where(row == 0, level_index[0].astype(jnp.float32), theirs)


def third_kernel(codes, early, before, part_strip, late, _, stats, strip, wide, square):
    strip[:, 0 : early.shape[0]] = part_strip[...]
    add_rows(codes, [early], late, before, stats, strip, wide, square)
    stats[1 + CODES :, :] = jnp.zeros((stats.shape[0] - 1 - CODES, stats.shape[1]), jnp.float32)


def last_kernel(codes, early, middle, before, part_strip, late, keep, mail, strip, wide, square, send):
    _, x, core = position()
    block = late.shape[0]
    half = block // 4
    strip[:, 0 : before.shape[1]] = part_strip[...]
    stats = keep.at[half:, :]
    add_rows(codes, [early, middle], late, before, stats, strip, wide, square)
    stats[1 + CODES :, :] = jnp.zeros((stats.shape[0] - 1 - CODES, stats.shape[1]), jnp.float32)
    keep[0:half, :] = strip[spot(core, half), :]
    send[0:half, :] = strip[spot(1 - core, half), :]
    send[half:, :] = stats[...]
    left, right = swapped(send, block)
    send[:, -3 * block : -2 * block] = left
    send[:, -block:] = right
    mail[0:half, :] = send[0:half, -3 * block :]
    mail[half:, :] = jnp.zeros((24, 3 * block), jnp.float32)
    for band, (low, high) in enumerate(((0, 3), (3, 6), (6, 8))):
        mail[half + 8 * band : half + 8 * band + 8, 0 : (high - low) * block] = send[
            half:, low * block : high * block
        ]


def counted(*levels):
    row = lax.broadcasted_iota(jnp.int32, (8, 1), 0).astype(jnp.float32) - 1.0
    found = [ref[ref.shape[0] - 8 + i : ref.shape[0] - 7 + i, 0:1] for ref in levels for i in (0, 1)]
    return sum(jnp.where(row == level, 1.0, 0.0) for level in found)


class Half:
    def __init__(self, own, width, codes, box, count, turned):
        _, x, core = position()
        rows = box.shape[0] - 8
        self.codes, self.width, self.count = codes, width, count
        self.gram, self.stats = box.at[0:rows, :], box.at[rows : rows + 8, :]
        own = spot(own, 4 * rows)
        beta, weight, stats = self.lines(own)
        row = lax.broadcasted_iota(jnp.int32, stats.shape, 0)
        inner = (row > 0) & (row <= CODES)
        lse = jnp.where(inner, count * (beta * stats[0:1] + jnp.log(stats)), 0.0)
        lse = jnp.sum(lse, axis=0, keepdims=True)
        turned[0] = jnp.where(inner, weight, jnp.where(row == 0, stats, lse)).T
        turned[1] = (beta * LOG2E).T
        mine = spot(2 * x + core, rows)
        lead, base = turned[0, mine, :], turned[1, mine, :]
        self.top, self.lse = lead[:, 0:1], lead[:, 7:8]
        self.weight = [lead[:, 1 + c : 2 + c] for c in range(CODES)]
        self.bases = base[:, 6:7], base[:, 5:6]

    def lines(self, cols):
        stats = self.stats[:, cols]
        row = lax.broadcasted_iota(jnp.int32, stats.shape, 0)
        code = self.codes[:, cols].astype(jnp.float32)
        beta = jnp.exp2(0.5 * (code - (row.astype(jnp.float32) - 1.0))) / jnp.sqrt(
            jnp.float32(self.width)
        )
        stats = jnp.where((row > CODES), 1.0, stats)
        return beta, self.count * beta / jnp.where(row == 0, 1.0, stats), stats

    def part(self, cols):
        gram = self.gram[:, cols]
        beta, weight, stats = self.lines(cols)
        by_row = sum(v * w for v, w in zip(powers(gram - self.top, *self.bases), self.weight))
        e = powers(gram - stats[0:1], beta[6:7] * LOG2E, beta[5:6] * LOG2E)
        by_col = sum(v * weight[1 + c : 2 + c] for c, v in enumerate(e))
        return by_row, by_row + by_col


def product(a, b):
    return jnp.dot(a, b, preferred_element_type=jnp.float32)


def store_loss(gap, difference, out):
    out[...] = jnp.broadcast_to(gap + difference, (gap.shape[0], 128)).T[0:1, :]


def half_kernel(width, codes, keep, level, their_level, by_row, both, lse, turned):
    half = Half(0, width, codes, keep, counted(level, their_level), turned)
    for col in range(0, codes.shape[1], 128):
        cols = pl.ds(col, 128)
        by_row[:, cols], both[:, cols] = half.part(cols)
    lse[...] = jnp.broadcast_to(half.lse, lse.shape)


def mix_kernel(
    codes, keep, mail, level, their_level, by_row, both, lse, early, middle, late, sooner, later,
    out, loss, turned, mix, recv
):
    share, block = out.shape[0], 4 * out.shape[0]
    recv[0:share, 0 : 5 * block] = their_level[0:share, :]
    recv[0:share, 5 * block :] = mail[0:share, :]
    for band, (low, high) in enumerate(((0, 3), (3, 6), (6, 8))):
        recv[share:, low * block : high * block] = mail[
            share + 8 * band : share + 8 * band + 8, 0 : (high - low) * block
        ]
    half = Half(0, out.shape[1], codes, recv, counted(level, their_level), turned)
    student = position()[2] == 1
    sign = jnp.where(student, 1.0, -1.0)
    rows = by_row.shape[0]
    gap = jnp.zeros((rows, 128), jnp.float32)
    for col in range(0, codes.shape[1], 128):
        cols = pl.ds(col, 128)
        their_row, their_both = half.part(cols)
        mix[:, cols] = ((WEIGHT * sign) * (both[:, cols] - their_both)).astype(jnp.bfloat16)
        p_row = jnp.where(student, their_row, by_row[:, cols])
        gap = gap + p_row * (recv[0:rows, cols] - keep[0:rows, cols])
    gap = jnp.sum(gap, axis=1, keepdims=True)
    store_loss(sign * gap, sign * (lse[:, 0:1] - half.lse), loss)

    def against(*parts):
        row, total = 0, None
        for part in parts:
            term = product(mix[:, row : row + part.shape[0]], part[...])
            row, total = row + part.shape[0], term if total is None else total + term
        out[...] = total

    @pl.when(student)
    def _():
        against(early, middle, late)

    @pl.when(jnp.logical_not(student))
    def _():
        against(sooner, later)


def wide_mix_kernel(codes, s_box, t_box, level, their_level, student, out, loss, turned):
    total, width = student.shape
    own, count = lax.axis_index("batch"), counted(level, their_level)
    s = Half(own, width, codes, s_box, count, turned.at[0:2])
    t = Half(own, width, codes, t_box, count, turned.at[2:4])
    span, rows = min(SPAN, total), out.shape[0]

    def step(i, carry):
        cols = at(i, span)
        (_, q), (p_row, p) = s.part(cols), t.part(cols)
        gap = jnp.sum(p_row * (t_box[0:rows, cols] - s_box[0:rows, cols]), axis=1, keepdims=True)
        mix = (WEIGHT * (q - p)).astype(jnp.bfloat16)
        return carry[0] + product(mix, student[cols, :]), carry[1] + gap

    zero = jnp.zeros((rows, width), jnp.float32), jnp.zeros((rows, 1), jnp.float32)
    out[...], gap = lax.fori_loop(0, total // span, step, zero)
    store_loss(gap, s.lse - t.lse, loss)


def call(kernel, shapes, scratch, limit, *args):
    return pl.pallas_call(
        kernel,
        out_shape=shapes,
        in_specs=[SMEM if a.shape == (1,) else VMEM for a in args],
        out_specs=[VMEM] * len(shapes),
        scratch_shapes=scratch,
        compiler_params=pltpu.CompilerParams(vmem_limit_bytes=limit << 20),
    )(*args)


def room(rows, cols):
    return [pltpu.VMEM((rows, cols), jnp.float32), pltpu.VMEM((rows, 8), jnp.float32)]


def join(parts, *behind):
    def kernel(*refs):
        row = 0
        for part in refs[: len(parts)]:
            refs[-1][row : row + part.shape[0], :] = part[...]
            row += part.shape[0]

    dims = sum(p.shape[0] for p in parts), parts[0].shape[1]
    return call(kernel, [shape(*dims, dtype=parts[0].dtype)], [], 16, *parts, *behind)[0]


def shape(*dims, dtype=jnp.float32):
    return jax.ShapeDtypeStruct(dims, dtype)


def shards(mesh, embeddings, spread_code, level_index):
    block, width = embeddings.shape[1:]
    batches, parts = mesh.shape["batch"], mesh.shape["temp"]
    total = block * batches
    me, part = lax.axis_index("batch"), lax.axis_index("temp")
    x, core = part // 2, part % 2
    rows, half = block // 2, block // 4

    def send(a, to):
        pairs = []
        for b in range(batches):
            for t in range(parts):
                there = to(b, t // 2, t % 2)
                pairs.append((b * parts + t, there[0] * parts + there[1] * 2 + there[2]))
        return lax.ppermute(a, ALL, pairs)

    over_core = lambda b, x, c: (b, x, 1 - c)
    over_x = lambda b, x, c: (b, 1 - x, c)
    u = lax.dynamic_index_in_dim(embeddings, core, 0, keepdims=False)
    out_shapes = [shape(half, width), shape(1, half)]
    codes = spread_code[None, :]

    if batches != 8 or parts != 4:
        whole = lax.all_gather(u, "batch", axis=0, tiled=True)
        theirs = send(level_index, over_x)
        stats, strip = call(
            functools.partial(first_kernel, False),
            [shape(8, total), shape(rows, total)],
            [pltpu.VMEM((1, total, TILE), jnp.float32)],
            56,
            codes,
            whole,
        )
        level = jnp.stack([level_index, theirs] + [theirs] * 6).astype(jnp.float32)
        level = jnp.broadcast_to(level, (8, 128))
        share = lambda c: lax.dynamic_slice_in_dim(strip, c * half, half)
        keep = jnp.concatenate([share(core), stats])
        recv = send(jnp.concatenate([share(1 - core), stats]), over_core)
        student = jnp.where(core == 1, whole, send(whole, over_core))
        out, loss = call(
            wide_mix_kernel,
            out_shapes,
            [pltpu.VMEM((4, block, 8), jnp.float32)],
            56,
            codes,
            jnp.where(core == 1, keep, recv),
            jnp.where(core == 1, recv, keep),
            level,
            send(level, over_core),
            student,
        )
        return out, loss[0]

    near = lambda b, x, c: (b ^ 2, x, c)
    far = lambda b, x, c: (b ^ 4, x, c)
    over_y = lambda b, x, c: (b ^ 1, x, c)
    turn = lambda b, x, c: (over_y if c else over_x)(b, x, c)
    return_turn = lambda b, x, c: (over_x if c else over_y)(b, x, c)
    level = jnp.broadcast_to(level_index.astype(jnp.bfloat16), (16, width))
    f = send(lax.dynamic_slice_in_dim(u, x * rows, rows, 0), far)
    n = send(u, near)
    y = send(u, over_y)
    g = send(f, near)
    ny = send(join([y], g), near)
    fa = send(join([f, level]), turn)
    fb = send(join([f, fa[:rows], level], g), return_turn)
    ga = send(g, turn)
    sooner = send(join([join([u, n]), y, f, g], fa), over_core)
    some, head = 4 * block, 6 * block
    codes, a_stats, a_strip, a_rows = call(
        functools.partial(first_kernel, True),
        [
            shape(1, total, dtype=jnp.int32),
            shape(8, some),
            shape(rows, some),
            shape(some, width, dtype=jnp.bfloat16),
        ],
        [pltpu.VMEM((some // TILE, some, TILE), jnp.float32)],
        16,
        codes,
        u,
        n,
        y,
        f,
        g,
    )
    gb = send(join([g, ga], sooner, a_stats), return_turn)
    b_stats, b_strip, b_rows, levels = call(
        second_kernel,
        [
            shape(8, head),
            shape(rows, head),
            shape(head, width, dtype=jnp.bfloat16),
            shape(half + 8, 5 * block),
        ],
        room(head - some, head),
        16,
        codes,
        a_rows,
        a_stats,
        a_strip,
        level_index,
        fa,
        fb,
        ga,
    )
    their_levels = send(levels, over_core)
    c_stats, c_strip = call(
        third_kernel,
        [shape(8, total - block), shape(rows, total - block)],
        room(block, total - block),
        16,
        codes,
        b_rows,
        b_stats,
        b_strip,
        ny,
        their_levels,
    )
    later = send(
        join([b_rows[some : some + 3 * rows], gb[:rows], ny, ga, gb[rows:]], c_stats), over_core
    )
    keep, mail = call(
        last_kernel,
        [shape(half + 8, total), shape(half + 24, 3 * block)],
        [pltpu.VMEM((rows, total), jnp.float32)]
        + room(block, total)
        + [pltpu.VMEM((half + 8, total), jnp.float32)],
        16,
        codes,
        b_rows,
        ny,
        c_stats,
        c_strip,
        gb,
    )
    recv = send(mail, over_core)
    by_row, both, lse = call(
        functools.partial(half_kernel, width),
        [shape(half, total), shape(half, total), shape(half, 8)],
        [pltpu.VMEM((2, block, 8), jnp.float32)],
        16,
        codes,
        keep,
        levels,
        their_levels,
    )
    out, loss = call(
        mix_kernel,
        out_shapes,
        [pltpu.VMEM((2, block, 8), jnp.float32), pltpu.VMEM((half, total), jnp.bfloat16), pltpu.VMEM((half + 8, total), jnp.float32)],
        16,
        codes,
        keep,
        recv,
        levels,
        their_levels,
        by_row,
        both,
        lse,
        b_rows,
        ny,
        gb,
        sooner,
        later,
    )
    return out, loss[0]


def solution(mesh):
    in_specs = (P(None, "batch", None), P(), P("temp"))
    out_specs = (P(("batch", "temp"), None), P(("batch", "temp")))
    return jax.shard_map(
        functools.partial(shards, mesh),
        mesh=mesh,
        in_specs=in_specs,
        out_specs=out_specs,
        check_vma=False,
    )
```
